32 devices in a mesh: grp: 4 (over y, x), blk: 8 (over z, core).
Axes of the slice: x: 2, y: 2, z: 4, core: 2. Of those that a mesh axis runs over, the one named last changes fastest.
Arguments:
- raw_blocks: bfloat16 [16, 24, 64, 256], P('blk', 'grp'), may hold values from -1.5 to 1.5
- metric_factor: bfloat16 [256, 256], replicated, may hold values from -0.375 to 0.375
- sig_list: int32 [16, 24], P('blk', 'grp'), may hold values from 0 to 15, as said below
- live_count: int32 [16, 4], P('blk', 'grp'), may hold values from 1 to 6, as said below
Outputs:
- exchange: float32 [1024, 1024], P('blk', 'grp')
The draws below stay inside these ranges and needn't reach their ends.
Inputs may be any that keep to these rules, and one draw needn't show every extreme that they name: `sig_list`: the 6 slots of one row block in one group name distinct orbital blocks. `live_count`: for every group, each aligned run of 2 row blocks holds a row block with all 6 slots live.
All inputs are finite; a program needn't handle non-finite values.
Results may differ from the reference program's by a relative error of at most 0.0011.
Values may be sent and summed in bfloat16 or wider, within the bound.
A program may use at most 64 MiB of HBM per device.

```python
import jax
import jax.numpy as jnp
from jax import lax

BS = 64
S = 6
MB = 2
NOB_DEV = 16
AUX = 256
NB = 16
N_GRP = 4


def draw_sig_list(key, part):
    scores = jax.random.randint(key, (NB, N_GRP, NOB_DEV), 0, 1048576)
    scores = scores * NOB_DEV + jnp.arange(NOB_DEV, dtype=jnp.int32)[None, None, :]
    order = jnp.argsort(scores, axis=-1, stable=True).astype(jnp.int32)
    return order[:, :, :S].reshape(NB, N_GRP * S)


def draw_live_count(key, part):
    counts = jax.random.randint(jax.random.fold_in(key, 11), (NB, N_GRP), 1, S + 1)
    picked = jax.random.randint(jax.random.fold_in(key, 12), (NB // MB, N_GRP), 0, MB)
    within = (jnp.arange(NB, dtype=jnp.int32) % MB)[:, None]
    full_row = within == jnp.repeat(picked, MB, axis=0)
    return jnp.where(full_row, S, counts).astype(jnp.int32)


def steps_of(rng, extent, cuts, low, largest):
    def one(axis_at, parts):
        heights = jax.random.uniform(jax.random.fold_in(jax.random.fold_in(rng, 6), axis_at), (parts,), jnp.float32, low / len(cuts), largest / len(cuts))
        return jnp.repeat(jnp.exp(heights), extent[axis_at] // parts).reshape((-1,) + (1,) * (len(extent) - axis_at - 1))

    factor_of = one(*cuts[0])
    for cut in cuts[1:]:
        factor_of = factor_of * one(*cut)
    return factor_of


def bell_draw(key, extent, spread, most, cuts=(), kind=jnp.bfloat16):
    values = spread * jax.random.normal(key, extent, jnp.float32)
    if cuts:
        values = values * steps_of(key, extent, cuts, -0.22, 0.18)
    return jnp.clip(values, -most, most).astype(kind)


def setup_inputs(seed: int = 0) -> dict:
    keys = jax.random.split(jax.random.key(seed), 5)
    raw_blocks = bell_draw(keys[0], (NB, N_GRP * S, BS, AUX), 0.25, 1.5, ((0, 8), (1, 4)))
    metric_factor = bell_draw(keys[1], (AUX, AUX), AUX ** -0.5, 0.375)
    sig_list = draw_sig_list(jax.random.fold_in(keys[4], 71), 0)
    live_count = draw_live_count(jax.random.fold_in(keys[4], 71), 0)
    return dict(raw_blocks=raw_blocks, metric_factor=metric_factor, sig_list=sig_list, live_count=live_count)


def reference(raw_blocks, metric_factor, sig_list, live_count):
    block_count = raw_blocks.shape[0]
    slot_index = jnp.arange(N_GRP * S, dtype=jnp.int32)
    group_of = slot_index // S
    live_mask = (slot_index % S)[None, :] < live_count[:, group_of]
    product = jnp.einsum('mjua,ab->mjub', raw_blocks.astype(jnp.float32), metric_factor.astype(jnp.float32), precision=lax.Precision.HIGHEST)
    contracted = (product * live_mask[:, :, None, None].astype(jnp.float32)).astype(jnp.bfloat16)
    total = jnp.zeros((block_count * BS, block_count * BS), jnp.float32)

    def add_group(total, group_index):
        group_x = lax.dynamic_slice_in_dim(contracted, (group_index * S).astype(jnp.int32), S, 1).astype(jnp.float32)
        group_ids = lax.dynamic_slice_in_dim(sig_list, (group_index * S).astype(jnp.int32), S, 1)
        one_hot = (group_ids[:, :, None] == jnp.arange(NOB_DEV, dtype=jnp.int32)[None, None, :]).astype(jnp.float32)
        dense = jnp.einsum('msn,msua->muna', one_hot, group_x, precision=lax.Precision.HIGHEST)
        flat = dense.reshape(block_count * BS, NOB_DEV * AUX)
        partial_sum = jnp.dot(flat, flat.T, precision=lax.Precision.HIGHEST, preferred_element_type=jnp.float32)
        return total + partial_sum, None

    total, unused = lax.scan(add_group, total, jnp.arange(N_GRP, dtype=jnp.int32))
    return 0.25 * total
```

```python
import functools

import jax
import jax.numpy as jnp
from jax import lax
from jax.experimental import pallas as pl
from jax.experimental.pallas import tpu as pltpu
from jax.sharding import PartitionSpec as P

NOB_DEV = 16
MESH = pl.DeviceIdType.MESH
CUTS = 2
LOW, HIGH = 0, 1


def both(*conditions):
    return functools.reduce(jnp.logical_and, conditions)


def kernel(
    chips, groups, raw_hbm, metric_hbm, sig_hbm, live, out,
    raw, metric, sig_vec, sig_own, xs, own, dense, ids_vec, ids, acc, red, half_sum, swap,
    in_sem, id_send, id_recv, id_local, chain_send, chain_recv, share_send, share_recv,
    red_send, red_recv, swap_send, swap_recv,
):
    row_blocks, slots, width, aux = raw_hbm.shape
    part = aux // 2
    rows = row_blocks * width
    cut_rows = slots * width // CUTS
    blk, grp = lax.axis_index("blk"), lax.axis_index("grp")
    chip, core = lax.div(blk, 2), lax.rem(blk, 2)
    sibling = 1 - core
    last = chips - 1

    def contributes(at, to):
        return jnp.logical_not(
            jnp.logical_or(both(at == 0, to == 1), both(at == last, to == last - 1))
        )

    def up_valid(source):
        return both(source >= 0, contributes(chip, source))

    def down_valid(source):
        return both(source <= last, contributes(chip, source))

    def chain_copy(source, half, m, cut, to_chip):
        piece = xs.at[core, source, half, m, pl.ds(cut * cut_rows, cut_rows)]
        return pltpu.make_async_remote_copy(
            src_ref=piece, dst_ref=piece,
            send_sem=chain_send.at[source, half, m, cut],
            recv_sem=chain_recv.at[source, half, m, cut],
            device_id={"blk": to_chip * 2 + core, "grp": grp}, device_id_type=MESH,
        )

    def share_copy(from_core, source, half, m):
        piece = xs.at[from_core, source, half, m]
        return pltpu.make_async_remote_copy(
            src_ref=piece, dst_ref=piece,
            send_sem=share_send.at[source, half, m], recv_sem=share_recv.at[source, half, m],
            device_id={"blk": chip * 2 + sibling, "grp": grp}, device_id_type=MESH,
        )

    def id_copy(slot, to_blk):
        return pltpu.make_async_remote_copy(
            src_ref=sig_vec, dst_ref=ids_vec.at[slot],
            send_sem=id_send.at[to_blk], recv_sem=id_recv.at[slot],
            device_id={"blk": to_blk, "grp": grp}, device_id_type=MESH,
        )

    def red_copy(slot, to_grp):
        return pltpu.make_async_remote_copy(
            src_ref=acc.at[to_grp], dst_ref=red.at[slot],
            send_sem=red_send.at[to_grp], recv_sem=red_recv.at[slot],
            device_id={"blk": blk, "grp": to_grp}, device_id_type=MESH,
        )

    def swap_copy(to_core, slot):
        return pltpu.make_async_remote_copy(
            src_ref=half_sum.at[to_core], dst_ref=swap.at[slot],
            send_sem=swap_send.at[to_core], recv_sem=swap_recv.at[slot],
            device_id={"blk": grp * 2 + to_core, "grp": chip}, device_id_type=MESH,
        )

    loads = [
        pltpu.make_async_copy(source, target, in_sem.at[index])
        for index, (source, target) in enumerate(
            ((raw_hbm, raw), (metric_hbm, metric), (sig_hbm, sig_vec), (sig_hbm, sig_own))
        )
    ]
    for load in loads:
        load.start()

    barrier = pltpu.get_barrier_semaphore()

    def greet_blk(other, carry):
        @pl.when(other != blk)
        def _():
            pl.semaphore_signal(
                barrier, inc=1, device_id={"blk": other, "grp": grp}, device_id_type=MESH
            )
        return carry

    def greet_grp(other, carry):
        @pl.when(other != grp)
        def _():
            pl.semaphore_signal(
                barrier, inc=1, device_id={"blk": blk, "grp": other}, device_id_type=MESH
            )
        return carry

    lax.fori_loop(0, 2 * chips, greet_blk, 0)
    lax.fori_loop(0, groups, greet_grp, 0)

    @pl.when(chip != grp)
    def _():
        for other in range(2):
            pl.semaphore_signal(
                barrier, inc=1, device_id={"blk": grp * 2 + other, "grp": chip}, device_id_type=MESH
            )

    for load in loads:
        load.wait()

    slot_of_row = lax.broadcasted_iota(jnp.int32, (slots * width, aux), 0) // width
    for m in range(row_blocks):
        product = jnp.dot(
            raw[m].reshape(slots * width, aux), metric[...], preferred_element_type=jnp.float32
        )
        kept = jnp.where(slot_of_row < live[0, m], product, 0.0).astype(jnp.bfloat16)
        for half in range(2):
            piece = kept[:, half * part : (half + 1) * part]
            xs[core, chip, half, m] = piece
            for s in range(slots):
                own[half, m, s] = piece[s * width : (s + 1) * width]
            own[half, m, slots] = jnp.zeros((width, part), jnp.bfloat16)
    ids_vec[blk] = sig_vec[...]

    pl.semaphore_wait(barrier, 2 * chips + groups - 2 + jnp.where(chip != grp, 2, 0))

    def send_ids(other, carry):
        @pl.when(other != blk)
        def _():
            id_copy(blk, other).start()
        return carry

    lax.fori_loop(0, 2 * chips, send_ids, 0)

    own_up = both(chip < last - 1)
    own_down = both(chip > 1)
    for m in range(row_blocks):
        for cut in range(CUTS):
            @pl.when(own_up)
            def _():
                chain_copy(chip, LOW, m, cut, chip + 1).start()

            @pl.when(own_down)
            def _():
                chain_copy(chip, HIGH, m, cut, chip - 1).start()

    for half in range(2):
        for m in range(row_blocks):
            share_copy(core, chip, half, m).start()

    for m in range(row_blocks):
        for n in range(NOB_DEV):
            at = jnp.int32(slots)
            for s in range(slots):
                at = jnp.where(sig_own[m, s] == n, s, at)
            for half in range(2):
                dense[half, n, m * width : (m + 1) * width, :] = own[half, m, at]

    acc[...] = jnp.zeros_like(acc)

    def wait_ids(other, carry):
        @pl.when(other != blk)
        def _():
            id_copy(other, other).wait_recv()
        return carry

    lax.fori_loop(0, 2 * chips, wait_ids, 0)
    to_scalar = pltpu.make_async_copy(ids_vec, ids, id_local)
    to_scalar.start()
    to_scalar.wait()

    def add_products(from_core, source, half, m):
        block = jnp.concatenate(
            [xs[from_core, source, half, m, s * width : (s + 1) * width, :] for s in range(slots)],
            axis=1,
        )
        chosen = jnp.concatenate(
            [dense[half, ids[source * 2 + from_core, m, s]] for s in range(slots)], axis=1
        )
        here = pl.ds(pl.multiple_of(m * width, width), width)
        acc[source, from_core, here, :] += lax.dot_general(
            block, chosen, (((1,), (1,)), ((), ())), preferred_element_type=jnp.float32
        )

    def send_partial(source):
        @pl.when(source != grp)
        def _():
            red_copy(grp, source).start()

    for half in range(2):
        for m in range(row_blocks):
            add_products(core, chip, half, m)

    for end, first, second, to_chip in ((0, LOW, HIGH, 1), (last, HIGH, LOW, last - 1)):
        @pl.when(chip == end)
        def _():
            for m in range(row_blocks):
                for cut in range(CUTS):
                    chain_copy(chip, first, m, cut, to_chip).wait_send()
                    chain_copy(chip, second, m, cut, to_chip).start()

    def arrive(source, half, m, onward, to_chip):
        for cut in range(CUTS):
            chain_copy(source, half, m, cut, chip).wait_recv()

            if onward is not None:
                @pl.when(onward)
                def _():
                    chain_copy(source, half, m, cut, to_chip).start()

        share_copy(core, source, half, m).start()

    def use(source, half, m):
        add_products(core, source, half, m)
        share_copy(sibling, source, half, m).wait_recv()
        add_products(sibling, source, half, m)

    def routes(step):
        below, above = chip - step, chip + step
        return (
            (up_valid(below), below, LOW, both(chip < last), chip + 1),
            (down_valid(above), above, HIGH, both(chip > 0), chip - 1),
            (both(step == 2, chip == 1), 0, HIGH, None, None),
            (both(step == 2, chip == last - 1), last, LOW, None, None),
        )

    def take_in(turn):
        step, m = lax.div(turn, row_blocks) + 1, lax.rem(turn, row_blocks)
        for valid, source, half, onward, to_chip in routes(step):
            @pl.when(valid)
            def _():
                arrive(source, half, m, onward, to_chip)

    def multiply(turn):
        step, m = lax.div(turn, row_blocks) + 1, lax.rem(turn, row_blocks)
        for index, (valid, source, half, onward, to_chip) in enumerate(routes(step)):
            @pl.when(valid)
            def _():
                use(source, half, m)

            whole = both(valid, m == row_blocks - 1)
            if index < 2:
                from_end = both(step == 1, source == (0, last)[index])
                whole = both(whole, jnp.logical_not(from_end))

            @pl.when(whole)
            def _():
                send_partial(source)

    def one_turn(turn, carry):
        @pl.when(turn < (chips - 1) * row_blocks)
        def _():
            take_in(turn)

        @pl.when(turn == 0)
        def _():
            for half in range(2):
                for m in range(row_blocks):
                    share_copy(sibling, chip, half, m).wait_recv()
                    add_products(sibling, chip, half, m)
            send_partial(chip)

        @pl.when(turn > 0)
        def _():
            multiply(turn - 1)

        return carry

    lax.fori_loop(0, (chips - 1) * row_blocks + 1, one_turn, 0)

    mine = contributes(chip, grp)
    theirs = both(chip != grp, contributes(grp, chip))

    @pl.when(mine)
    def _():
        for core_at in range(2):
            half_sum[core_at] = acc[grp, core_at]

        def add_group(other, carry):
            @pl.when(other != grp)
            def _():
                red_copy(other, grp).wait_recv()
                for core_at in range(2):
                    half_sum[core_at] += red[other, core_at]
            return carry

        lax.fori_loop(0, groups, add_group, 0)

        @pl.when(chip != grp)
        def _():
            for core_at in range(2):
                swap_copy(core_at, core).start()

        for core_at in range(2):
            out[:, core_at * rows : (core_at + 1) * rows] = 0.25 * half_sum[core_at].T

    @pl.when(theirs)
    def _():
        for core_at in range(2):
            swap_copy(core_at, core_at).wait_recv()

    @pl.when(both(mine, theirs))
    def _():
        for core_at in range(2):
            out[:, core_at * rows : (core_at + 1) * rows] += 0.25 * swap[core_at]

    @pl.when(jnp.logical_not(mine))
    def _():
        for core_at in range(2):
            out[:, core_at * rows : (core_at + 1) * rows] = 0.25 * swap[core_at]

    def done_ids(other, carry):
        @pl.when(other != blk)
        def _():
            id_copy(blk, other).wait_send()
        return carry

    lax.fori_loop(0, 2 * chips, done_ids, 0)

    def done_source(source, carry):
        low_here = jnp.logical_or(
            source == chip,
            jnp.logical_or(
                both(source < chip, contributes(chip, source)),
                both(source == last, chip == last - 1),
            ),
        )
        high_here = jnp.logical_or(
            source == chip,
            jnp.logical_or(
                both(source > chip, contributes(chip, source)),
                both(source == 0, chip == 1),
            ),
        )
        low_sent = jnp.logical_or(
            jnp.where(source == chip, both(own_up, chip > 0), both(source < chip, chip < last)),
            both(source == chip, chip == last),
        )
        high_sent = jnp.logical_or(
            jnp.where(source == chip, both(own_down, chip < last), both(source > chip, chip > 0)),
            both(source == chip, chip == 0),
        )
        for half, here, sent in ((LOW, low_here, low_sent), (HIGH, high_here, high_sent)):
            @pl.when(here)
            def _():
                for m in range(row_blocks):
                    share_copy(core, source, half, m).wait_send()

            @pl.when(sent)
            def _():
                for m in range(row_blocks):
                    for cut in range(CUTS):
                        chain_copy(source, half, m, cut, chip).wait_send()

        @pl.when(both(source != grp, contributes(chip, source)))
        def _():
            red_copy(grp, source).wait_send()

        return carry

    lax.fori_loop(0, chips, done_source, 0)

    @pl.when(both(mine, chip != grp))
    def _():
        for core_at in range(2):
            swap_copy(core_at, core).wait_send()


def exchange_kernel(raw_blocks, metric_factor, sig_list, live_count):
    row_blocks, slots, width, aux = raw_blocks.shape
    blks, groups = lax.axis_size("blk"), lax.axis_size("grp")
    chips = blks // 2
    rows, part = row_blocks * width, aux // 2
    vmem = pl.BlockSpec(memory_space=pltpu.VMEM)
    hbm = pl.BlockSpec(memory_space=pltpu.HBM)
    smem = pl.BlockSpec(memory_space=pltpu.SMEM)
    dma = pltpu.SemaphoreType.DMA
    return pl.pallas_call(
        functools.partial(kernel, chips, groups),
        out_shape=jax.ShapeDtypeStruct((rows, 2 * rows), jnp.float32),
        in_specs=[hbm, hbm, hbm, smem],
        out_specs=vmem,
        scratch_shapes=[
            pltpu.VMEM(raw_blocks.shape, jnp.bfloat16),
            pltpu.VMEM(metric_factor.shape, jnp.bfloat16),
            pltpu.VMEM(sig_list.shape, jnp.int32),
            pltpu.SMEM(sig_list.shape, jnp.int32),
            pltpu.VMEM((2, chips, 2, row_blocks, slots * width, part), jnp.bfloat16),
            pltpu.VMEM((2, row_blocks, slots + 1, width, part), jnp.bfloat16),
            pltpu.VMEM((2, NOB_DEV, rows, part), jnp.bfloat16),
            pltpu.VMEM((blks, row_blocks, slots), jnp.int32),
            pltpu.SMEM((blks, row_blocks, slots), jnp.int32),
            pltpu.VMEM((chips, 2, rows, rows), jnp.float32),
            pltpu.VMEM((groups, 2, rows, rows), jnp.float32),
            pltpu.VMEM((2, rows, rows), jnp.float32),
            pltpu.VMEM((2, rows, rows), jnp.float32),
            dma((4,)), dma((blks,)), dma((blks,)), dma,
            dma((chips, 2, row_blocks, CUTS)), dma((chips, 2, row_blocks, CUTS)),
            dma((chips, 2, row_blocks)), dma((chips, 2, row_blocks)),
            dma((groups,)), dma((groups,)), dma((2,)), dma((2,)),
        ],
        compiler_params=pltpu.CompilerParams(
            collective_id=0, has_side_effects=True, vmem_limit_bytes=60 * 2**20
        ),
        cost_estimate=pl.CostEstimate(
            flops=2 * rows * 2 * rows * chips * slots * aux, bytes_accessed=2**20, transcendentals=0
        ),
    )(raw_blocks, metric_factor, sig_list, live_count.T)


def solution(mesh):
    placed = (P("blk", "grp", None, None), P(), P("blk", "grp"), P("blk", "grp"))
    return jax.shard_map(
        exchange_kernel, mesh=mesh, in_specs=placed, out_specs=P("blk", "grp"), check_vma=False
    )
```

```python
import functools

import jax
import jax.numpy as jnp
from jax import lax
from jax.experimental import pallas as pl
from jax.experimental.pallas import tpu as pltpu
from jax.sharding import PartitionSpec as P

NOB_DEV = 16
MESH = pl.DeviceIdType.MESH
CUTS = 2
LOW, HIGH = 0, 1


def both(*conditions):
    return functools.reduce(jnp.logical_and, conditions)


def kernel(
    chips, groups, raw_hbm, metric_hbm, sig_hbm, live, out,
    raw, metric, sig_vec, sig_own, xs, own, dense, ids_vec, ids, acc, red, half_sum, kept_sum, swap,
    in_sem, id_send, id_recv, id_local, chain_send, chain_recv, share_send, share_recv,
    red_send, red_recv, keep_send, keep_recv, swap_send, swap_recv,
):
    row_blocks, slots, width, aux = raw_hbm.shape
    part = aux // 2
    rows = row_blocks * width
    cut_rows = slots * width // CUTS
    blk, grp = lax.axis_index("blk"), lax.axis_index("grp")
    chip, core = lax.div(blk, 2), lax.rem(blk, 2)
    sibling = 1 - core
    last = chips - 1

    def contributes(at, to):
        return jnp.logical_not(
            jnp.logical_or(both(at == 0, to == 1), both(at == last, to == last - 1))
        )

    def up_valid(source):
        return both(source >= 0, contributes(chip, source))

    def down_valid(source):
        return both(source <= last, contributes(chip, source))

    def chain_copy(source, half, m, cut, to_chip):
        piece = xs.at[core, source, half, m, pl.ds(cut * cut_rows, cut_rows)]
        return pltpu.make_async_remote_copy(
            src_ref=piece, dst_ref=piece,
            send_sem=chain_send.at[source, half, m, cut],
            recv_sem=chain_recv.at[source, half, m, cut],
            device_id={"blk": to_chip * 2 + core, "grp": grp}, device_id_type=MESH,
        )

    def share_copy(from_core, source, half, m):
        piece = xs.at[from_core, source, half, m]
        return pltpu.make_async_remote_copy(
            src_ref=piece, dst_ref=piece,
            send_sem=share_send.at[source, half, m], recv_sem=share_recv.at[source, half, m],
            device_id={"blk": chip * 2 + sibling, "grp": grp}, device_id_type=MESH,
        )

    def id_copy(slot, to_blk):
        return pltpu.make_async_remote_copy(
            src_ref=sig_vec, dst_ref=ids_vec.at[slot],
            send_sem=id_send.at[to_blk], recv_sem=id_recv.at[slot],
            device_id={"blk": to_blk, "grp": grp}, device_id_type=MESH,
        )

    share = 2 * rows // groups
    per_core = groups // 2

    def rows_of(group):
        return pl.ds(pl.multiple_of(group * share, share), share)

    def red_copy(source, slot, to_grp):
        return pltpu.make_async_remote_copy(
            src_ref=acc.at[source, rows_of(to_grp)], dst_ref=red.at[source, slot],
            send_sem=red_send.at[source, to_grp], recv_sem=red_recv.at[source, slot],
            device_id={"blk": blk, "grp": to_grp}, device_id_type=MESH,
        )

    def keep_copy(source, slot):
        return pltpu.make_async_remote_copy(
            src_ref=half_sum.at[source], dst_ref=kept_sum.at[rows_of(slot)],
            send_sem=keep_send.at[source], recv_sem=keep_recv.at[slot],
            device_id={"blk": blk, "grp": source}, device_id_type=MESH,
        )

    def swap_copy(source, from_core, slot):
        return pltpu.make_async_remote_copy(
            src_ref=half_sum.at[source], dst_ref=swap.at[from_core, rows_of(slot)],
            send_sem=swap_send.at[source], recv_sem=swap_recv.at[from_core, slot],
            device_id={"blk": source * 2 + lax.div(grp, per_core), "grp": chip},
            device_id_type=MESH,
        )

    loads = [
        pltpu.make_async_copy(source, target, in_sem.at[index])
        for index, (source, target) in enumerate(
            ((raw_hbm, raw), (metric_hbm, metric), (sig_hbm, sig_vec), (sig_hbm, sig_own))
        )
    ]
    for load in loads:
        load.start()

    barrier = pltpu.get_barrier_semaphore()

    def greet_blk(other, carry):
        @pl.when(other != blk)
        def _():
            pl.semaphore_signal(
                barrier, inc=1, device_id={"blk": other, "grp": grp}, device_id_type=MESH
            )
        return carry

    def greet_grp(other, carry):
        @pl.when(other != grp)
        def _():
            pl.semaphore_signal(
                barrier, inc=1, device_id={"blk": blk, "grp": other}, device_id_type=MESH
            )
        return carry

    lax.fori_loop(0, 2 * chips, greet_blk, 0)
    lax.fori_loop(0, groups, greet_grp, 0)

    @pl.when(chip != grp)
    def _():
        for slot in range(per_core):
            group = core * per_core + slot

            @pl.when(group != grp)
            def _():
                for other in range(2):
                    pl.semaphore_signal(
                        barrier, inc=1, device_id={"blk": grp * 2 + other, "grp": group},
                        device_id_type=MESH,
                    )

    for load in loads:
        load.wait()

    slot_of_row = lax.broadcasted_iota(jnp.int32, (slots * width, aux), 0) // width
    for m in range(row_blocks):
        product = jnp.dot(
            raw[m].reshape(slots * width, aux), metric[...], preferred_element_type=jnp.float32
        )
        kept = jnp.where(slot_of_row < live[0, m], product, 0.0).astype(jnp.bfloat16)
        for half in range(2):
            piece = kept[:, half * part : (half + 1) * part]
            xs[core, chip, half, m] = piece
    ids_vec[blk] = sig_vec[...]

    pl.semaphore_wait(barrier, 2 * chips + groups - 2 + jnp.where(chip != grp, chips - 1, 0))

    def send_ids(other, carry):
        @pl.when(other != blk)
        def _():
            id_copy(blk, other).start()
        return carry

    lax.fori_loop(0, 2 * chips, send_ids, 0)

    own_up = both(chip < last - 1)
    own_down = both(chip > 1)
    for m in range(row_blocks):
        for cut in range(CUTS):
            @pl.when(own_up)
            def _():
                chain_copy(chip, LOW, m, cut, chip + 1).start()

            @pl.when(own_down)
            def _():
                chain_copy(chip, HIGH, m, cut, chip - 1).start()

    for half in range(2):
        for m in range(row_blocks):
            share_copy(core, chip, half, m).start()

    for half in range(2):
        for s in range(slots):
            block = jnp.concatenate(
                [
                    xs[core, chip, half, m, s * width : (s + 1) * width, :]
                    for m in range(row_blocks)
                ],
                axis=0,
            )
            own[half, s] = block.astype(jnp.float32).T.astype(jnp.bfloat16)
        own[half, slots] = jnp.zeros((part, rows), jnp.bfloat16)

    row_block_of = lax.broadcasted_iota(jnp.int32, (part, rows), 1) // width
    for n in range(NOB_DEV):
        places = []
        for m in range(row_blocks):
            at = jnp.int32(slots)
            for s in range(slots):
                at = jnp.where(sig_own[m, s] == n, s, at)
            places.append(at)
        for half in range(2):
            chosen = own[half, places[0]]
            for m in range(1, row_blocks):
                chosen = jnp.where(row_block_of == m, own[half, places[m]], chosen)
            dense[half, n] = chosen

    acc[...] = jnp.zeros_like(acc)

    def wait_ids(other, carry):
        @pl.when(other != blk)
        def _():
            id_copy(other, other).wait_recv()
        return carry

    lax.fori_loop(0, 2 * chips, wait_ids, 0)
    to_scalar = pltpu.make_async_copy(ids_vec, ids, id_local)
    to_scalar.start()
    to_scalar.wait()

    def add_products(from_core, source, half, m):
        block = jnp.concatenate(
            [xs[from_core, source, half, m, s * width : (s + 1) * width, :] for s in range(slots)],
            axis=1,
        )
        chosen = jnp.concatenate(
            [dense[half, ids[source * 2 + from_core, m, s]] for s in range(slots)], axis=0
        )
        here = pl.ds(pl.multiple_of(from_core * rows + m * width, width), width)
        acc[source, here, :] += jnp.dot(block, chosen, preferred_element_type=jnp.float32)

    def send_partial(source):
        def to_group(other, carry):
            @pl.when(other != grp)
            def _():
                red_copy(source, grp, other).start()
            return carry

        lax.fori_loop(0, groups, to_group, 0)

    def finish(source):
        def add_group(other, total):
            red_copy(source, other, other).wait_recv()
            return total + red[source, other]

        total = lax.fori_loop(0, grp, add_group, acc[source, rows_of(grp), :])
        half_sum[source] = lax.fori_loop(grp + 1, groups, add_group, total)

        @pl.when(source != chip)
        def _():
            swap_copy(source, core, lax.rem(grp, per_core)).start()

        @pl.when(source != grp)
        def _():
            keep_copy(source, grp).start()

        @pl.when(source == grp)
        def _():
            kept_sum[rows_of(grp), :] = half_sum[source]

    for half in range(2):
        for m in range(row_blocks):
            add_products(core, chip, half, m)

    for end, first, second, to_chip in ((0, LOW, HIGH, 1), (last, HIGH, LOW, last - 1)):
        @pl.when(chip == end)
        def _():
            for m in range(row_blocks):
                for cut in range(CUTS):
                    chain_copy(chip, first, m, cut, to_chip).wait_send()
                    chain_copy(chip, second, m, cut, to_chip).start()

    def arrive(source, half, m, onward, to_chip):
        for cut in range(CUTS):
            chain_copy(source, half, m, cut, chip).wait_recv()

            if onward is not None:
                @pl.when(onward)
                def _():
                    chain_copy(source, half, m, cut, to_chip).start()

        share_copy(core, source, half, m).start()

    def use(source, half, m):
        add_products(core, source, half, m)
        share_copy(sibling, source, half, m).wait_recv()
        add_products(sibling, source, half, m)

    def routes(step):
        below, above = chip - step, chip + step
        return (
            (up_valid(below), below, LOW, both(chip < last), chip + 1),
            (down_valid(above), above, HIGH, both(chip > 0), chip - 1),
            (both(step == 2, chip == 1), 0, HIGH, None, None),
            (both(step == 2, chip == last - 1), last, LOW, None, None),
        )

    def take_in(turn):
        step, m = lax.div(turn, row_blocks) + 1, lax.rem(turn, row_blocks)
        for valid, source, half, onward, to_chip in routes(step):
            @pl.when(valid)
            def _():
                arrive(source, half, m, onward, to_chip)

    def multiply(turn):
        step, m = lax.div(turn, row_blocks) + 1, lax.rem(turn, row_blocks)
        for index, (valid, source, half, onward, to_chip) in enumerate(routes(step)):
            @pl.when(valid)
            def _():
                use(source, half, m)

            whole = both(valid, m == row_blocks - 1)
            if index < 2:
                from_end = both(step == 1, source == (0, last)[index])
                whole = both(whole, jnp.logical_not(from_end))

            @pl.when(whole)
            def _():
                send_partial(source)

    def one_turn(turn, carry):
        @pl.when(turn < (chips - 1) * row_blocks)
        def _():
            take_in(turn)

        @pl.when(turn == 0)
        def _():
            for half in range(2):
                for m in range(row_blocks):
                    share_copy(sibling, chip, half, m).wait_recv()
                    add_products(sibling, chip, half, m)
            send_partial(chip)

        @pl.when(turn > 0)
        def _():
            multiply(turn - 1)

        return carry

    lax.fori_loop(0, (chips - 1) * row_blocks + 1, one_turn, 0)

    finish(chip)

    def finish_distance(step, carry):
        for source in (chip - step, chip + step):
            @pl.when(both(source >= 0, source <= last, contributes(chip, source)))
            def _():
                finish(source)

        return carry

    lax.fori_loop(1, chips, finish_distance, 0)

    mine = contributes(chip, grp)
    theirs = both(chip != grp, contributes(grp, chip))

    @pl.when(mine)
    def _():
        def wait_kept(other, carry):
            @pl.when(other != grp)
            def _():
                keep_copy(other, other).wait_recv()
            return carry

        lax.fori_loop(0, groups, wait_kept, 0)
        for core_at in range(2):
            here = slice(core_at * rows, (core_at + 1) * rows)
            out[:, here] = 0.25 * kept_sum[here, :].T

    @pl.when(theirs)
    def _():
        for core_at in range(2):
            for slot in range(per_core):
                swap_copy(chip, core_at, slot).wait_recv()

    @pl.when(both(mine, theirs))
    def _():
        for core_at in range(2):
            out[:, core_at * rows : (core_at + 1) * rows] += 0.25 * swap[core_at]

    @pl.when(jnp.logical_not(mine))
    def _():
        for core_at in range(2):
            out[:, core_at * rows : (core_at + 1) * rows] = 0.25 * swap[core_at]

    def done_ids(other, carry):
        @pl.when(other != blk)
        def _():
            id_copy(blk, other).wait_send()
        return carry

    lax.fori_loop(0, 2 * chips, done_ids, 0)

    def done_source(source, carry):
        low_here = jnp.logical_or(
            source == chip,
            jnp.logical_or(
                both(source < chip, contributes(chip, source)),
                both(source == last, chip == last - 1),
            ),
        )
        high_here = jnp.logical_or(
            source == chip,
            jnp.logical_or(
                both(source > chip, contributes(chip, source)),
                both(source == 0, chip == 1),
            ),
        )
        low_sent = jnp.logical_or(
            jnp.where(source == chip, both(own_up, chip > 0), both(source < chip, chip < last)),
            both(source == chip, chip == last),
        )
        high_sent = jnp.logical_or(
            jnp.where(source == chip, both(own_down, chip < last), both(source > chip, chip > 0)),
            both(source == chip, chip == 0),
        )
        for half, here, sent in ((LOW, low_here, low_sent), (HIGH, high_here, high_sent)):
            @pl.when(here)
            def _():
                for m in range(row_blocks):
                    share_copy(core, source, half, m).wait_send()

            @pl.when(sent)
            def _():
                for m in range(row_blocks):
                    for cut in range(CUTS):
                        chain_copy(source, half, m, cut, chip).wait_send()

        @pl.when(contributes(chip, source))
        def _():
            def done_group(other, inner):
                @pl.when(other != grp)
                def _():
                    red_copy(source, grp, other).wait_send()
                return inner

            lax.fori_loop(0, groups, done_group, 0)

            @pl.when(source != chip)
            def _():
                swap_copy(source, core, 0).wait_send()

            @pl.when(source != grp)
            def _():
                keep_copy(source, grp).wait_send()

        return carry

    lax.fori_loop(0, chips, done_source, 0)


def exchange_kernel(raw_blocks, metric_factor, sig_list, live_count):
    row_blocks, slots, width, aux = raw_blocks.shape
    blks, groups = lax.axis_size("blk"), lax.axis_size("grp")
    chips = blks // 2
    rows, part = row_blocks * width, aux // 2
    share = 2 * rows // groups
    vmem = pl.BlockSpec(memory_space=pltpu.VMEM)
    hbm = pl.BlockSpec(memory_space=pltpu.HBM)
    smem = pl.BlockSpec(memory_space=pltpu.SMEM)
    dma = pltpu.SemaphoreType.DMA
    return pl.pallas_call(
        functools.partial(kernel, chips, groups),
        out_shape=jax.ShapeDtypeStruct((rows, 2 * rows), jnp.float32),
        in_specs=[hbm, hbm, hbm, smem],
        out_specs=vmem,
        scratch_shapes=[
            pltpu.VMEM(raw_blocks.shape, jnp.bfloat16),
            pltpu.VMEM(metric_factor.shape, jnp.bfloat16),
            pltpu.VMEM(sig_list.shape, jnp.int32),
            pltpu.SMEM(sig_list.shape, jnp.int32),
            pltpu.VMEM((2, chips, 2, row_blocks, slots * width, part), jnp.bfloat16),
            pltpu.VMEM((2, slots + 1, part, rows), jnp.bfloat16),
            pltpu.VMEM((2, NOB_DEV, part, rows), jnp.bfloat16),
            pltpu.VMEM((blks, row_blocks, slots), jnp.int32),
            pltpu.SMEM((blks, row_blocks, slots), jnp.int32),
            pltpu.VMEM((chips, 2 * rows, rows), jnp.float32),
            pltpu.VMEM((chips, groups, share, rows), jnp.float32),
            pltpu.VMEM((chips, share, rows), jnp.float32),
            pltpu.VMEM((2 * rows, rows), jnp.float32),
            pltpu.VMEM((2, rows, rows), jnp.float32),
            dma((4,)), dma((blks,)), dma((blks,)), dma,
            dma((chips, 2, row_blocks, CUTS)), dma((chips, 2, row_blocks, CUTS)),
            dma((chips, 2, row_blocks)), dma((chips, 2, row_blocks)),
            dma((chips, groups)), dma((chips, groups)), dma((chips,)), dma((groups,)),
            dma((chips,)), dma((2, groups // 2)),
        ],
        compiler_params=pltpu.CompilerParams(
            collective_id=0, has_side_effects=True, vmem_limit_bytes=60 * 2**20
        ),
        cost_estimate=pl.CostEstimate(
            flops=2 * rows * 2 * rows * chips * slots * aux, bytes_accessed=2**20, transcendentals=0
        ),
    )(raw_blocks, metric_factor, sig_list, live_count.T)


def solution(mesh):
    placed = (P("blk", "grp", None, None), P(), P("blk", "grp"), P("blk", "grp"))
    return jax.shard_map(
        exchange_kernel, mesh=mesh, in_specs=placed, out_specs=P("blk", "grp"), check_vma=False
    )
```

```python
import functools

import jax
import jax.numpy as jnp
from jax import lax
from jax.experimental import pallas as pl
from jax.experimental.pallas import tpu as pltpu
from jax.sharding import PartitionSpec as P

NOB_DEV = 16
MESH = pl.DeviceIdType.MESH
CUTS = 2
LOW, HIGH = 0, 1


def both(*conditions):
    return functools.reduce(jnp.logical_and, conditions)


def kernel(
    chips, groups, raw_hbm, metric_hbm, sig_hbm, live, out,
    raw, metric, sig_vec, sig_own, xs, own, dense, ids_vec, ids, acc, red, half_sum, kept_sum, swap,
    in_sem, id_send, id_recv, id_local, chain_send, chain_recv, share_send, share_recv,
    red_send, red_recv, keep_send, keep_recv, swap_send, swap_recv,
):
    row_blocks, slots, width, aux = raw_hbm.shape
    part = aux // 2
    rows = row_blocks * width
    cut_rows = slots * width // CUTS
    blk, grp = lax.axis_index("blk"), lax.axis_index("grp")
    chip, core = lax.div(blk, 2), lax.rem(blk, 2)
    sibling = 1 - core
    last = chips - 1

    def contributes(at, to):
        return jnp.logical_not(
            jnp.logical_or(both(at == 0, to == 1), both(at == last, to == last - 1))
        )

    def up_valid(source):
        return both(source >= 0, contributes(chip, source))

    def down_valid(source):
        return both(source <= last, contributes(chip, source))

    def chain_copy(source, half, m, cut, to_chip):
        piece = xs.at[core, source, half, m, pl.ds(cut * cut_rows, cut_rows)]
        return pltpu.make_async_remote_copy(
            src_ref=piece, dst_ref=piece,
            send_sem=chain_send.at[source, half, m, cut],
            recv_sem=chain_recv.at[source, half, m, cut],
            device_id={"blk": to_chip * 2 + core, "grp": grp}, device_id_type=MESH,
        )

    def share_copy(from_core, source, half, m):
        piece = xs.at[from_core, source, half, m]
        return pltpu.make_async_remote_copy(
            src_ref=piece, dst_ref=piece,
            send_sem=share_send.at[source, half, m], recv_sem=share_recv.at[source, half, m],
            device_id={"blk": chip * 2 + sibling, "grp": grp}, device_id_type=MESH,
        )

    def id_copy(slot, to_blk):
        return pltpu.make_async_remote_copy(
            src_ref=sig_vec, dst_ref=ids_vec.at[slot],
            send_sem=id_send.at[to_blk], recv_sem=id_recv.at[slot],
            device_id={"blk": to_blk, "grp": grp}, device_id_type=MESH,
        )

    share = 2 * rows // groups
    per_core = groups // 2

    def rows_of(group):
        return pl.ds(pl.multiple_of(group * share, share), share)

    def red_copy(source, slot, to_grp):
        return pltpu.make_async_remote_copy(
            src_ref=acc.at[source, rows_of(to_grp)], dst_ref=red.at[source, slot],
            send_sem=red_send.at[source, to_grp], recv_sem=red_recv.at[source, slot],
            device_id={"blk": blk, "grp": to_grp}, device_id_type=MESH,
        )

    def keep_copy(source, slot):
        return pltpu.make_async_remote_copy(
            src_ref=half_sum.at[source], dst_ref=kept_sum.at[rows_of(slot)],
            send_sem=keep_send.at[source], recv_sem=keep_recv.at[slot],
            device_id={"blk": blk, "grp": source}, device_id_type=MESH,
        )

    def swap_copy(source, from_core, slot):
        return pltpu.make_async_remote_copy(
            src_ref=half_sum.at[source], dst_ref=swap.at[from_core, rows_of(slot)],
            send_sem=swap_send.at[source], recv_sem=swap_recv.at[from_core, slot],
            device_id={"blk": source * 2 + lax.div(grp, per_core), "grp": chip},
            device_id_type=MESH,
        )

    loads = [
        pltpu.make_async_copy(source, target, in_sem.at[index])
        for index, (source, target) in enumerate(
            ((raw_hbm, raw), (metric_hbm, metric), (sig_hbm, sig_vec), (sig_hbm, sig_own))
        )
    ]
    for load in loads:
        load.start()

    barrier = pltpu.get_barrier_semaphore()

    def greet_blk(other, carry):
        @pl.when(other != blk)
        def _():
            pl.semaphore_signal(
                barrier, inc=1, device_id={"blk": other, "grp": grp}, device_id_type=MESH
            )
        return carry

    def greet_grp(other, carry):
        @pl.when(other != grp)
        def _():
            pl.semaphore_signal(
                barrier, inc=1, device_id={"blk": blk, "grp": other}, device_id_type=MESH
            )
        return carry

    lax.fori_loop(0, 2 * chips, greet_blk, 0)
    lax.fori_loop(0, groups, greet_grp, 0)

    @pl.when(chip != grp)
    def _():
        for slot in range(per_core):
            group = core * per_core + slot

            @pl.when(group != grp)
            def _():
                for other in range(2):
                    pl.semaphore_signal(
                        barrier, inc=1, device_id={"blk": grp * 2 + other, "grp": group},
                        device_id_type=MESH,
                    )

    for load in loads:
        load.wait()

    own_up = both(chip < last - 1)
    own_down = both(chip > 1)
    slot_of_row = lax.broadcasted_iota(jnp.int32, (slots * width, aux), 0) // width
    for m in range(row_blocks):
        product = jnp.dot(
            raw[m].reshape(slots * width, aux), metric[...], preferred_element_type=jnp.float32
        )
        kept = jnp.where(slot_of_row < live[0, m], product, 0.0).astype(jnp.bfloat16)
        for half in range(2):
            xs[core, chip, half, m] = kept[:, half * part : (half + 1) * part]

        if m == 0:
            pl.semaphore_wait(
                barrier, 2 * chips + groups - 2 + jnp.where(chip != grp, chips - 1, 0)
            )

        for cut in range(CUTS):
            @pl.when(own_up)
            def _():
                chain_copy(chip, LOW, m, cut, chip + 1).start()

            @pl.when(own_down)
            def _():
                chain_copy(chip, HIGH, m, cut, chip - 1).start()

    def send_ids(other, carry):
        @pl.when(other != blk)
        def _():
            id_copy(blk, other).start()
        return carry

    lax.fori_loop(0, 2 * chips, send_ids, 0)
    ids_vec[blk] = sig_vec[...]

    for half in range(2):
        for m in range(row_blocks):
            share_copy(core, chip, half, m).start()

    for half in range(2):
        for s in range(slots):
            block = jnp.concatenate(
                [
                    xs[core, chip, half, m, s * width : (s + 1) * width, :]
                    for m in range(row_blocks)
                ],
                axis=0,
            )
            own[half, s] = block.astype(jnp.float32).T.astype(jnp.bfloat16)
        own[half, slots] = jnp.zeros((part, rows), jnp.bfloat16)

    row_block_of = lax.broadcasted_iota(jnp.int32, (part, rows), 1) // width
    for n in range(NOB_DEV):
        places = []
        for m in range(row_blocks):
            at = jnp.int32(slots)
            for s in range(slots):
                at = jnp.where(sig_own[m, s] == n, s, at)
            places.append(at)
        for half in range(2):
            chosen = own[half, places[0]]
            for m in range(1, row_blocks):
                chosen = jnp.where(row_block_of == m, own[half, places[m]], chosen)
            dense[half, n] = chosen

    acc[...] = jnp.zeros_like(acc)

    def add_products(from_core, source, half, m):
        block = jnp.concatenate(
            [xs[from_core, source, half, m, s * width : (s + 1) * width, :] for s in range(slots)],
            axis=1,
        )
        chosen = jnp.concatenate(
            [dense[half, ids[source * 2 + from_core, m, s]] for s in range(slots)], axis=0
        )
        here = pl.ds(pl.multiple_of(from_core * rows + m * width, width), width)
        acc[source, here, :] += jnp.dot(block, chosen, preferred_element_type=jnp.float32)

    def send_partial(source):
        def to_group(other, carry):
            @pl.when(other != grp)
            def _():
                red_copy(source, grp, other).start()
            return carry

        lax.fori_loop(0, groups, to_group, 0)

    def finish(source):
        def add_group(other, total):
            red_copy(source, other, other).wait_recv()
            return total + red[source, other]

        total = lax.fori_loop(0, grp, add_group, acc[source, rows_of(grp), :])
        half_sum[source] = lax.fori_loop(grp + 1, groups, add_group, total)

        @pl.when(source != chip)
        def _():
            swap_copy(source, core, lax.rem(grp, per_core)).start()

        @pl.when(source != grp)
        def _():
            keep_copy(source, grp).start()

        @pl.when(source == grp)
        def _():
            kept_sum[rows_of(grp), :] = half_sum[source]

    for end, first, second, to_chip in ((0, LOW, HIGH, 1), (last, HIGH, LOW, last - 1)):
        @pl.when(chip == end)
        def _():
            for m in range(row_blocks):
                for cut in range(CUTS):
                    chain_copy(chip, first, m, cut, to_chip).wait_send()
                    chain_copy(chip, second, m, cut, to_chip).start()

    def arrive(source, half, m, onward, to_chip):
        for cut in range(CUTS):
            chain_copy(source, half, m, cut, chip).wait_recv()

            if onward is not None:
                @pl.when(onward)
                def _():
                    chain_copy(source, half, m, cut, to_chip).start()

        share_copy(core, source, half, m).start()

    def use(source, half, m):
        add_products(core, source, half, m)
        share_copy(sibling, source, half, m).wait_recv()
        add_products(sibling, source, half, m)

    def routes(step):
        below, above = chip - step, chip + step
        return (
            (up_valid(below), below, LOW, both(chip < last), chip + 1),
            (down_valid(above), above, HIGH, both(chip > 0), chip - 1),
            (both(step == 2, chip == 1), 0, HIGH, None, None),
            (both(step == 2, chip == last - 1), last, LOW, None, None),
        )

    def take_in(turn):
        step, m = lax.div(turn, row_blocks) + 1, lax.rem(turn, row_blocks)
        for valid, source, half, onward, to_chip in routes(step):
            @pl.when(valid)
            def _():
                arrive(source, half, m, onward, to_chip)

    def multiply(turn):
        step, m = lax.div(turn, row_blocks) + 1, lax.rem(turn, row_blocks)
        for index, (valid, source, half, onward, to_chip) in enumerate(routes(step)):
            @pl.when(valid)
            def _():
                use(source, half, m)

            whole = both(valid, m == row_blocks - 1)
            if index < 2:
                from_end = both(step == 1, source == (0, last)[index])
                whole = both(whole, jnp.logical_not(from_end))

            @pl.when(whole)
            def _():
                send_partial(source)

    def finish_distance(step):
        @pl.when(step == 0)
        def _():
            finish(chip)

        below, above = chip - step, chip + step
        from_ends = (both(step == 2, chip == 1), both(step == 2, chip == last - 1))
        for valid, source, end, from_end in (
            (up_valid(below), below, 0, from_ends[0]), (down_valid(above), above, last, from_ends[1])
        ):
            late = both(step == 1, source == end)

            @pl.when(both(valid, step > 0, jnp.logical_not(late)))
            def _():
                finish(source)

            @pl.when(from_end)
            def _():
                finish(end)

    def one_turn(turn, carry):
        @pl.when(turn < (chips - 1) * row_blocks)
        def _():
            take_in(turn)

        @pl.when(turn == 0)
        def _():
            @functools.partial(lax.fori_loop, 0, 2 * chips, init_val=0)
            def _(other, carry):
                @pl.when(other != blk)
                def _():
                    id_copy(other, other).wait_recv()
                return carry

            to_scalar = pltpu.make_async_copy(ids_vec, ids, id_local)
            to_scalar.start()
            to_scalar.wait()
            for half in range(2):
                for m in range(row_blocks):
                    add_products(core, chip, half, m)
            for half in range(2):
                for m in range(row_blocks):
                    share_copy(sibling, chip, half, m).wait_recv()
                    add_products(sibling, chip, half, m)
            send_partial(chip)

        @pl.when(turn > 0)
        def _():
            multiply(turn - 1)

        @pl.when(both(turn > 0, lax.rem(turn, row_blocks) == 0))
        def _():
            finish_distance(lax.div(turn, row_blocks) - 1)

        return carry

    lax.fori_loop(0, (chips - 1) * row_blocks + 1, one_turn, 0)
    finish_distance(chips - 1)

    mine = contributes(chip, grp)
    theirs = both(chip != grp, contributes(grp, chip))

    @pl.when(mine)
    def _():
        def wait_kept(other, carry):
            @pl.when(other != grp)
            def _():
                keep_copy(other, other).wait_recv()
            return carry

        lax.fori_loop(0, groups, wait_kept, 0)
        for core_at in range(2):
            here = slice(core_at * rows, (core_at + 1) * rows)
            out[:, here] = 0.25 * kept_sum[here, :].T

    @pl.when(theirs)
    def _():
        for core_at in range(2):
            for slot in range(per_core):
                swap_copy(chip, core_at, slot).wait_recv()

    @pl.when(both(mine, theirs))
    def _():
        for core_at in range(2):
            out[:, core_at * rows : (core_at + 1) * rows] += 0.25 * swap[core_at]

    @pl.when(jnp.logical_not(mine))
    def _():
        for core_at in range(2):
            out[:, core_at * rows : (core_at + 1) * rows] = 0.25 * swap[core_at]

    def done_ids(other, carry):
        @pl.when(other != blk)
        def _():
            id_copy(blk, other).wait_send()
        return carry

    lax.fori_loop(0, 2 * chips, done_ids, 0)

    def done_source(source, carry):
        low_here = jnp.logical_or(
            source == chip,
            jnp.logical_or(
                both(source < chip, contributes(chip, source)),
                both(source == last, chip == last - 1),
            ),
        )
        high_here = jnp.logical_or(
            source == chip,
            jnp.logical_or(
                both(source > chip, contributes(chip, source)),
                both(source == 0, chip == 1),
            ),
        )
        low_sent = jnp.logical_or(
            jnp.where(source == chip, both(own_up, chip > 0), both(source < chip, chip < last)),
            both(source == chip, chip == last),
        )
        high_sent = jnp.logical_or(
            jnp.where(source == chip, both(own_down, chip < last), both(source > chip, chip > 0)),
            both(source == chip, chip == 0),
        )
        for half, here, sent in ((LOW, low_here, low_sent), (HIGH, high_here, high_sent)):
            @pl.when(here)
            def _():
                for m in range(row_blocks):
                    share_copy(core, source, half, m).wait_send()

            @pl.when(sent)
            def _():
                for m in range(row_blocks):
                    for cut in range(CUTS):
                        chain_copy(source, half, m, cut, chip).wait_send()

        @pl.when(contributes(chip, source))
        def _():
            def done_group(other, inner):
                @pl.when(other != grp)
                def _():
                    red_copy(source, grp, other).wait_send()
                return inner

            lax.fori_loop(0, groups, done_group, 0)

            @pl.when(source != chip)
            def _():
                swap_copy(source, core, 0).wait_send()

            @pl.when(source != grp)
            def _():
                keep_copy(source, grp).wait_send()

        return carry

    lax.fori_loop(0, chips, done_source, 0)


def exchange_kernel(raw_blocks, metric_factor, sig_list, live_count):
    row_blocks, slots, width, aux = raw_blocks.shape
    blks, groups = lax.axis_size("blk"), lax.axis_size("grp")
    chips = blks // 2
    rows, part = row_blocks * width, aux // 2
    share = 2 * rows // groups
    vmem = pl.BlockSpec(memory_space=pltpu.VMEM)
    hbm = pl.BlockSpec(memory_space=pltpu.HBM)
    smem = pl.BlockSpec(memory_space=pltpu.SMEM)
    dma = pltpu.SemaphoreType.DMA
    return pl.pallas_call(
        functools.partial(kernel, chips, groups),
        out_shape=jax.ShapeDtypeStruct((rows, 2 * rows), jnp.float32),
        in_specs=[hbm, hbm, hbm, smem],
        out_specs=vmem,
        scratch_shapes=[
            pltpu.VMEM(raw_blocks.shape, jnp.bfloat16),
            pltpu.VMEM(metric_factor.shape, jnp.bfloat16),
            pltpu.VMEM(sig_list.shape, jnp.int32),
            pltpu.SMEM(sig_list.shape, jnp.int32),
            pltpu.VMEM((2, chips, 2, row_blocks, slots * width, part), jnp.bfloat16),
            pltpu.VMEM((2, slots + 1, part, rows), jnp.bfloat16),
            pltpu.VMEM((2, NOB_DEV, part, rows), jnp.bfloat16),
            pltpu.VMEM((blks, row_blocks, slots), jnp.int32),
            pltpu.SMEM((blks, row_blocks, slots), jnp.int32),
            pltpu.VMEM((chips, 2 * rows, rows), jnp.float32),
            pltpu.VMEM((chips, groups, share, rows), jnp.float32),
            pltpu.VMEM((chips, share, rows), jnp.float32),
            pltpu.VMEM((2 * rows, rows), jnp.float32),
            pltpu.VMEM((2, rows, rows), jnp.float32),
            dma((4,)), dma((blks,)), dma((blks,)), dma,
            dma((chips, 2, row_blocks, CUTS)), dma((chips, 2, row_blocks, CUTS)),
            dma((chips, 2, row_blocks)), dma((chips, 2, row_blocks)),
            dma((chips, groups)), dma((chips, groups)), dma((chips,)), dma((groups,)),
            dma((chips,)), dma((2, groups // 2)),
        ],
        compiler_params=pltpu.CompilerParams(
            collective_id=0, has_side_effects=True, vmem_limit_bytes=60 * 2**20
        ),
        cost_estimate=pl.CostEstimate(
            flops=2 * rows * 2 * rows * chips * slots * aux, bytes_accessed=2**20, transcendentals=0
        ),
    )(raw_blocks, metric_factor, sig_list, live_count.T)


def solution(mesh):
    placed = (P("blk", "grp", None, None), P(), P("blk", "grp"), P("blk", "grp"))
    return jax.shard_map(
        exchange_kernel, mesh=mesh, in_specs=placed, out_specs=P("blk", "grp"), check_vma=False
    )
```

```python
import functools

import jax
import jax.numpy as jnp
from jax import lax
from jax.experimental import pallas as pl
from jax.experimental.pallas import tpu as pltpu
from jax.sharding import PartitionSpec as P

NOB_DEV = 16
MESH = pl.DeviceIdType.MESH
CUTS = 2
LOW, HIGH = 0, 1


def both(*conditions):
    return functools.reduce(jnp.logical_and, conditions)


def kernel(
    chips, groups, raw_hbm, metric_hbm, sig_hbm, live, out,
    raw, metric, sig_vec, sig_own, xs, own, dense, ids_vec, ids, acc, red, half_sum, kept_sum, swap,
    in_sem, id_send, id_recv, id_local, chain_send, chain_recv, share_send, share_recv,
    red_send, red_recv, keep_send, keep_recv, swap_send, swap_recv,
):
    row_blocks, slots, width, aux = raw_hbm.shape
    part = aux // 2
    rows = row_blocks * width
    cut_rows = slots * width // CUTS
    blk, grp = lax.axis_index("blk"), lax.axis_index("grp")
    chip, core = lax.div(blk, 2), lax.rem(blk, 2)
    sibling = 1 - core
    last = chips - 1

    def contributes(at, to):
        return jnp.logical_not(
            jnp.logical_or(both(at == 0, to == 1), both(at == last, to == last - 1))
        )

    def up_valid(source):
        return both(source >= 0, contributes(chip, source))

    def down_valid(source):
        return both(source <= last, contributes(chip, source))

    def chain_copy(source, half, m, cut, to_chip):
        piece = xs.at[core, source, half, m, pl.ds(cut * cut_rows, cut_rows)]
        return pltpu.make_async_remote_copy(
            src_ref=piece, dst_ref=piece,
            send_sem=chain_send.at[source, half, m, cut],
            recv_sem=chain_recv.at[source, half, m, cut],
            device_id={"blk": to_chip * 2 + core, "grp": grp}, device_id_type=MESH,
        )

    def share_copy(from_core, source, half, m):
        piece = xs.at[from_core, source, half, m]
        return pltpu.make_async_remote_copy(
            src_ref=piece, dst_ref=piece,
            send_sem=share_send.at[source, half, m], recv_sem=share_recv.at[source, half, m],
            device_id={"blk": chip * 2 + sibling, "grp": grp}, device_id_type=MESH,
        )

    def id_copy(slot, to_blk):
        return pltpu.make_async_remote_copy(
            src_ref=sig_vec, dst_ref=ids_vec.at[slot],
            send_sem=id_send.at[to_blk], recv_sem=id_recv.at[slot],
            device_id={"blk": to_blk, "grp": grp}, device_id_type=MESH,
        )

    share = 2 * rows // groups
    per_core = groups // 2

    def rows_of(group):
        return pl.ds(pl.multiple_of(group * share, share), share)

    def red_copy(source, slot, to_grp):
        return pltpu.make_async_remote_copy(
            src_ref=acc.at[source, rows_of(to_grp)], dst_ref=red.at[source, slot],
            send_sem=red_send.at[source, to_grp], recv_sem=red_recv.at[source, slot],
            device_id={"blk": blk, "grp": to_grp}, device_id_type=MESH,
        )

    def keep_copy(source, slot):
        return pltpu.make_async_remote_copy(
            src_ref=half_sum.at[source], dst_ref=kept_sum.at[rows_of(slot)],
            send_sem=keep_send.at[source], recv_sem=keep_recv.at[slot],
            device_id={"blk": blk, "grp": source}, device_id_type=MESH,
        )

    def swap_copy(source, from_core, slot):
        return pltpu.make_async_remote_copy(
            src_ref=half_sum.at[source], dst_ref=swap.at[from_core, rows_of(slot)],
            send_sem=swap_send.at[source], recv_sem=swap_recv.at[from_core, slot],
            device_id={"blk": source * 2 + lax.div(grp, per_core), "grp": chip},
            device_id_type=MESH,
        )

    loads = [
        pltpu.make_async_copy(source, target, in_sem.at[index])
        for index, (source, target) in enumerate(
            ((raw_hbm, raw), (metric_hbm, metric), (sig_hbm, sig_vec), (sig_hbm, sig_own))
        )
    ]
    for load in loads:
        load.start()

    barrier = pltpu.get_barrier_semaphore()

    def greet_blk(other, carry):
        @pl.when(other != blk)
        def _():
            pl.semaphore_signal(
                barrier, inc=1, device_id={"blk": other, "grp": grp}, device_id_type=MESH
            )
        return carry

    def greet_grp(other, carry):
        @pl.when(other != grp)
        def _():
            pl.semaphore_signal(
                barrier, inc=1, device_id={"blk": blk, "grp": other}, device_id_type=MESH
            )
        return carry

    lax.fori_loop(0, 2 * chips, greet_blk, 0)
    lax.fori_loop(0, groups, greet_grp, 0)

    @pl.when(chip != grp)
    def _():
        for slot in range(per_core):
            group = core * per_core + slot

            @pl.when(group != grp)
            def _():
                for other in range(2):
                    pl.semaphore_signal(
                        barrier, inc=1, device_id={"blk": grp * 2 + other, "grp": group},
                        device_id_type=MESH,
                    )

    for load in loads:
        load.wait()

    def send_ids(other, carry):
        @pl.when(other != blk)
        def _():
            id_copy(blk, other).start()
        return carry

    own_up = both(chip < last - 1)
    own_down = both(chip > 1)
    slot_of_row = lax.broadcasted_iota(jnp.int32, (slots * width, aux), 0) // width
    for m in range(row_blocks):
        product = jnp.dot(
            raw[m].reshape(slots * width, aux), metric[...], preferred_element_type=jnp.float32
        )
        kept = jnp.where(slot_of_row < live[0, m], product, 0.0).astype(jnp.bfloat16)
        for half in range(2):
            xs[core, chip, half, m] = kept[:, half * part : (half + 1) * part]

        if m == 0:
            pl.semaphore_wait(
                barrier, 2 * chips + groups - 2 + jnp.where(chip != grp, chips - 1, 0)
            )
            lax.fori_loop(0, 2 * chips, send_ids, 0)
            ids_vec[blk] = sig_vec[...]

        for cut in range(CUTS):
            @pl.when(own_up)
            def _():
                chain_copy(chip, LOW, m, cut, chip + 1).start()

            @pl.when(own_down)
            def _():
                chain_copy(chip, HIGH, m, cut, chip - 1).start()

    for half in range(2):
        for m in range(row_blocks):
            share_copy(core, chip, half, m).start()

    for half in range(2):
        for s in range(slots):
            block = jnp.concatenate(
                [
                    xs[core, chip, half, m, s * width : (s + 1) * width, :]
                    for m in range(row_blocks)
                ],
                axis=0,
            )
            own[half, s] = block.astype(jnp.float32).T.astype(jnp.bfloat16)
        own[half, slots] = jnp.zeros((part, rows), jnp.bfloat16)

    row_block_of = lax.broadcasted_iota(jnp.int32, (part, rows), 1) // width
    for n in range(NOB_DEV):
        places = []
        for m in range(row_blocks):
            at = jnp.int32(slots)
            for s in range(slots):
                at = jnp.where(sig_own[m, s] == n, s, at)
            places.append(at)
        for half in range(2):
            chosen = own[half, places[0]]
            for m in range(1, row_blocks):
                chosen = jnp.where(row_block_of == m, own[half, places[m]], chosen)
            dense[half, n] = chosen

    acc[...] = jnp.zeros_like(acc)

    def add_products(from_core, source, half, m):
        block = jnp.concatenate(
            [xs[from_core, source, half, m, s * width : (s + 1) * width, :] for s in range(slots)],
            axis=1,
        )
        chosen = jnp.concatenate(
            [dense[half, ids[source * 2 + from_core, m, s]] for s in range(slots)], axis=0
        )
        here = pl.ds(pl.multiple_of(from_core * rows + m * width, width), width)
        acc[source, here, :] += jnp.dot(block, chosen, preferred_element_type=jnp.float32)

    def send_partial(source):
        def to_group(other, carry):
            @pl.when(other != grp)
            def _():
                red_copy(source, grp, other).start()
            return carry

        lax.fori_loop(0, groups, to_group, 0)

    def finish(source):
        def add_group(other, total):
            red_copy(source, other, other).wait_recv()
            return total + red[source, other]

        total = lax.fori_loop(0, grp, add_group, acc[source, rows_of(grp), :])
        half_sum[source] = lax.fori_loop(grp + 1, groups, add_group, total)

        @pl.when(source != chip)
        def _():
            swap_copy(source, core, lax.rem(grp, per_core)).start()

        @pl.when(source != grp)
        def _():
            keep_copy(source, grp).start()

        @pl.when(source == grp)
        def _():
            kept_sum[rows_of(grp), :] = half_sum[source]

    for end, first, second, to_chip in ((0, LOW, HIGH, 1), (last, HIGH, LOW, last - 1)):
        @pl.when(chip == end)
        def _():
            for m in range(row_blocks):
                for cut in range(CUTS):
                    chain_copy(chip, first, m, cut, to_chip).wait_send()
                    chain_copy(chip, second, m, cut, to_chip).start()

    def arrive(source, half, m, onward, to_chip):
        for cut in range(CUTS):
            chain_copy(source, half, m, cut, chip).wait_recv()

            if onward is not None:
                @pl.when(onward)
                def _():
                    chain_copy(source, half, m, cut, to_chip).start()

        share_copy(core, source, half, m).start()

    def use(source, half, m):
        add_products(core, source, half, m)
        share_copy(sibling, source, half, m).wait_recv()
        add_products(sibling, source, half, m)

    def routes(step):
        below, above = chip - step, chip + step
        return (
            (up_valid(below), below, LOW, both(chip < last), chip + 1),
            (down_valid(above), above, HIGH, both(chip > 0), chip - 1),
            (both(step == 2, chip == 1), 0, HIGH, None, None),
            (both(step == 2, chip == last - 1), last, LOW, None, None),
        )

    def take_in(turn):
        step, m = lax.div(turn, row_blocks) + 1, lax.rem(turn, row_blocks)
        for valid, source, half, onward, to_chip in routes(step):
            @pl.when(valid)
            def _():
                arrive(source, half, m, onward, to_chip)

    def multiply(turn):
        step, m = lax.div(turn, row_blocks) + 1, lax.rem(turn, row_blocks)
        for index, (valid, source, half, onward, to_chip) in enumerate(routes(step)):
            @pl.when(valid)
            def _():
                use(source, half, m)

            whole = both(valid, m == row_blocks - 1)
            if index < 2:
                from_end = both(step == 1, source == (0, last)[index])
                whole = both(whole, jnp.logical_not(from_end))

            @pl.when(whole)
            def _():
                send_partial(source)

    def finish_distance(step):
        @pl.when(step == 0)
        def _():
            finish(chip)

        below, above = chip - step, chip + step
        from_ends = (both(step == 2, chip == 1), both(step == 2, chip == last - 1))
        for valid, source, end, from_end in (
            (up_valid(below), below, 0, from_ends[0]), (down_valid(above), above, last, from_ends[1])
        ):
            late = both(step == 1, source == end)

            @pl.when(both(valid, step > 0, jnp.logical_not(late)))
            def _():
                finish(source)

            @pl.when(from_end)
            def _():
                finish(end)

    def one_turn(turn, carry):
        @pl.when(turn < (chips - 1) * row_blocks)
        def _():
            take_in(turn)

        @pl.when(turn == 0)
        def _():
            @functools.partial(lax.fori_loop, 0, 2 * chips, init_val=0)
            def _(other, carry):
                @pl.when(other != blk)
                def _():
                    id_copy(other, other).wait_recv()
                return carry

            to_scalar = pltpu.make_async_copy(ids_vec, ids, id_local)
            to_scalar.start()
            to_scalar.wait()
            for half in range(2):
                for m in range(row_blocks):
                    add_products(core, chip, half, m)
            for half in range(2):
                for m in range(row_blocks):
                    share_copy(sibling, chip, half, m).wait_recv()
                    add_products(sibling, chip, half, m)
            send_partial(chip)

        @pl.when(turn > 0)
        def _():
            multiply(turn - 1)

        return carry

    lax.fori_loop(0, (chips - 1) * row_blocks + 1, one_turn, 0)

    @functools.partial(lax.fori_loop, 0, chips, init_val=0)
    def _(step, carry):
        finish_distance(step)
        return carry

    mine = contributes(chip, grp)
    theirs = both(chip != grp, contributes(grp, chip))

    @pl.when(mine)
    def _():
        def wait_kept(other, carry):
            @pl.when(other != grp)
            def _():
                keep_copy(other, other).wait_recv()
            return carry

        lax.fori_loop(0, groups, wait_kept, 0)
        for core_at in range(2):
            here = slice(core_at * rows, (core_at + 1) * rows)
            out[:, here] = 0.25 * kept_sum[here, :].T

    @pl.when(theirs)
    def _():
        for core_at in range(2):
            for slot in range(per_core):
                swap_copy(chip, core_at, slot).wait_recv()

    @pl.when(both(mine, theirs))
    def _():
        for core_at in range(2):
            out[:, core_at * rows : (core_at + 1) * rows] += 0.25 * swap[core_at]

    @pl.when(jnp.logical_not(mine))
    def _():
        for core_at in range(2):
            out[:, core_at * rows : (core_at + 1) * rows] = 0.25 * swap[core_at]

    def done_ids(other, carry):
        @pl.when(other != blk)
        def _():
            id_copy(blk, other).wait_send()
        return carry

    lax.fori_loop(0, 2 * chips, done_ids, 0)

    def done_source(source, carry):
        low_here = jnp.logical_or(
            source == chip,
            jnp.logical_or(
                both(source < chip, contributes(chip, source)),
                both(source == last, chip == last - 1),
            ),
        )
        high_here = jnp.logical_or(
            source == chip,
            jnp.logical_or(
                both(source > chip, contributes(chip, source)),
                both(source == 0, chip == 1),
            ),
        )
        low_sent = jnp.logical_or(
            jnp.where(source == chip, both(own_up, chip > 0), both(source < chip, chip < last)),
            both(source == chip, chip == last),
        )
        high_sent = jnp.logical_or(
            jnp.where(source == chip, both(own_down, chip < last), both(source > chip, chip > 0)),
            both(source == chip, chip == 0),
        )
        for half, here, sent in ((LOW, low_here, low_sent), (HIGH, high_here, high_sent)):
            @pl.when(here)
            def _():
                for m in range(row_blocks):
                    share_copy(core, source, half, m).wait_send()

            @pl.when(sent)
            def _():
                for m in range(row_blocks):
                    for cut in range(CUTS):
                        chain_copy(source, half, m, cut, chip).wait_send()

        @pl.when(contributes(chip, source))
        def _():
            def done_group(other, inner):
                @pl.when(other != grp)
                def _():
                    red_copy(source, grp, other).wait_send()
                return inner

            lax.fori_loop(0, groups, done_group, 0)

            @pl.when(source != chip)
            def _():
                swap_copy(source, core, 0).wait_send()

            @pl.when(source != grp)
            def _():
                keep_copy(source, grp).wait_send()

        return carry

    lax.fori_loop(0, chips, done_source, 0)


def exchange_kernel(raw_blocks, metric_factor, sig_list, live_count):
    row_blocks, slots, width, aux = raw_blocks.shape
    blks, groups = lax.axis_size("blk"), lax.axis_size("grp")
    chips = blks // 2
    rows, part = row_blocks * width, aux // 2
    share = 2 * rows // groups
    vmem = pl.BlockSpec(memory_space=pltpu.VMEM)
    hbm = pl.BlockSpec(memory_space=pltpu.HBM)
    smem = pl.BlockSpec(memory_space=pltpu.SMEM)
    dma = pltpu.SemaphoreType.DMA
    return pl.pallas_call(
        functools.partial(kernel, chips, groups),
        out_shape=jax.ShapeDtypeStruct((rows, 2 * rows), jnp.float32),
        in_specs=[hbm, hbm, hbm, smem],
        out_specs=vmem,
        scratch_shapes=[
            pltpu.VMEM(raw_blocks.shape, jnp.bfloat16),
            pltpu.VMEM(metric_factor.shape, jnp.bfloat16),
            pltpu.VMEM(sig_list.shape, jnp.int32),
            pltpu.SMEM(sig_list.shape, jnp.int32),
            pltpu.VMEM((2, chips, 2, row_blocks, slots * width, part), jnp.bfloat16),
            pltpu.VMEM((2, slots + 1, part, rows), jnp.bfloat16),
            pltpu.VMEM((2, NOB_DEV, part, rows), jnp.bfloat16),
            pltpu.VMEM((blks, row_blocks, slots), jnp.int32),
            pltpu.SMEM((blks, row_blocks, slots), jnp.int32),
            pltpu.VMEM((chips, 2 * rows, rows), jnp.float32),
            pltpu.VMEM((chips, groups, share, rows), jnp.float32),
            pltpu.VMEM((chips, share, rows), jnp.float32),
            pltpu.VMEM((2 * rows, rows), jnp.float32),
            pltpu.VMEM((2, rows, rows), jnp.float32),
            dma((4,)), dma((blks,)), dma((blks,)), dma,
            dma((chips, 2, row_blocks, CUTS)), dma((chips, 2, row_blocks, CUTS)),
            dma((chips, 2, row_blocks)), dma((chips, 2, row_blocks)),
            dma((chips, groups)), dma((chips, groups)), dma((chips,)), dma((groups,)),
            dma((chips,)), dma((2, groups // 2)),
        ],
        compiler_params=pltpu.CompilerParams(
            collective_id=0, has_side_effects=True, vmem_limit_bytes=56400000
        ),
        cost_estimate=pl.CostEstimate(
            flops=2 * rows * 2 * rows * chips * slots * aux, bytes_accessed=2**20, transcendentals=0
        ),
    )(raw_blocks, metric_factor, sig_list, live_count.T)


def solution(mesh):
    placed = (P("blk", "grp", None, None), P(), P("blk", "grp"), P("blk", "grp"))
    return jax.shard_map(
        exchange_kernel, mesh=mesh, in_specs=placed, out_specs=P("blk", "grp"), check_vma=False
    )
```

```python
import functools

import jax
import jax.numpy as jnp
from jax import lax
from jax.experimental import pallas as pl
from jax.experimental.pallas import tpu as pltpu
from jax.sharding import PartitionSpec as P

NOB_DEV = 16
MESH = pl.DeviceIdType.MESH
CUTS = 2
LOW, HIGH = 0, 1


def both(*conditions):
    return functools.reduce(jnp.logical_and, conditions)


def kernel(
    chips, groups, raw_hbm, metric_hbm, sig_hbm, live, out,
    raw, metric, sig_vec, sig_own, xs, own, dense, ids_vec, ids, acc, red, half_sum, kept_sum, swap,
    in_sem, id_send, id_recv, id_local, chain_send, chain_recv, share_send, share_recv,
    red_send, red_recv, keep_send, keep_recv, swap_send, swap_recv,
):
    row_blocks, slots, width, aux = raw_hbm.shape
    part = aux // 2
    rows = row_blocks * width
    cut_rows = slots * width // CUTS
    blk, grp = lax.axis_index("blk"), lax.axis_index("grp")
    chip, core = lax.div(blk, 2), lax.rem(blk, 2)
    sibling = 1 - core
    last = chips - 1

    def contributes(at, to):
        return jnp.logical_not(
            jnp.logical_or(both(at == 0, to == 1), both(at == last, to == last - 1))
        )

    def up_valid(source):
        return both(source >= 0, contributes(chip, source))

    def down_valid(source):
        return both(source <= last, contributes(chip, source))

    def chain_copy(source, half, m, cut, to_chip):
        piece = xs.at[core, source, half, m, pl.ds(cut * cut_rows, cut_rows)]
        return pltpu.make_async_remote_copy(
            src_ref=piece, dst_ref=piece,
            send_sem=chain_send.at[source, half, m, cut],
            recv_sem=chain_recv.at[source, half, m, cut],
            device_id={"blk": to_chip * 2 + core, "grp": grp}, device_id_type=MESH,
        )

    def share_copy(from_core, source, half, m):
        piece = xs.at[from_core, source, half, m]
        return pltpu.make_async_remote_copy(
            src_ref=piece, dst_ref=piece,
            send_sem=share_send.at[source, half, m], recv_sem=share_recv.at[source, half, m],
            device_id={"blk": chip * 2 + sibling, "grp": grp}, device_id_type=MESH,
        )

    def id_copy(slot, to_blk):
        return pltpu.make_async_remote_copy(
            src_ref=sig_vec, dst_ref=ids_vec.at[slot],
            send_sem=id_send.at[to_blk], recv_sem=id_recv.at[slot],
            device_id={"blk": to_blk, "grp": grp}, device_id_type=MESH,
        )

    share = 2 * rows // groups
    per_core = groups // 2

    def rows_of(group):
        return pl.ds(pl.multiple_of(group * share, share), share)

    def red_copy(source, slot, to_grp):
        return pltpu.make_async_remote_copy(
            src_ref=acc.at[source, rows_of(to_grp)], dst_ref=red.at[source, slot],
            send_sem=red_send.at[source, to_grp], recv_sem=red_recv.at[source, slot],
            device_id={"blk": blk, "grp": to_grp}, device_id_type=MESH,
        )

    def keep_copy(source, slot):
        return pltpu.make_async_remote_copy(
            src_ref=half_sum.at[source], dst_ref=kept_sum.at[rows_of(slot)],
            send_sem=keep_send.at[source], recv_sem=keep_recv.at[slot],
            device_id={"blk": blk, "grp": source}, device_id_type=MESH,
        )

    def swap_copy(source, from_core, slot):
        return pltpu.make_async_remote_copy(
            src_ref=half_sum.at[source], dst_ref=swap.at[from_core, rows_of(slot)],
            send_sem=swap_send.at[source], recv_sem=swap_recv.at[from_core, slot],
            device_id={"blk": source * 2 + lax.div(grp, per_core), "grp": chip},
            device_id_type=MESH,
        )

    loads = [
        pltpu.make_async_copy(source, target, in_sem.at[index])
        for index, (source, target) in enumerate(
            ((raw_hbm, raw), (metric_hbm, metric), (sig_hbm, sig_vec), (sig_hbm, sig_own))
        )
    ]
    for load in loads:
        load.start()

    barrier = pltpu.get_barrier_semaphore()

    def greet_blk(other, carry):
        @pl.when(other != blk)
        def _():
            pl.semaphore_signal(
                barrier, inc=1, device_id={"blk": other, "grp": grp}, device_id_type=MESH
            )
        return carry

    def greet_grp(other, carry):
        @pl.when(other != grp)
        def _():
            pl.semaphore_signal(
                barrier, inc=1, device_id={"blk": blk, "grp": other}, device_id_type=MESH
            )
        return carry

    lax.fori_loop(0, 2 * chips, greet_blk, 0)
    lax.fori_loop(0, groups, greet_grp, 0)

    @pl.when(chip != grp)
    def _():
        for slot in range(per_core):
            group = core * per_core + slot

            @pl.when(group != grp)
            def _():
                for other in range(2):
                    pl.semaphore_signal(
                        barrier, inc=1, device_id={"blk": grp * 2 + other, "grp": group},
                        device_id_type=MESH,
                    )

    for load in loads:
        load.wait()

    def send_ids(other, carry):
        @pl.when(other != blk)
        def _():
            id_copy(blk, other).start()
        return carry

    own_up = both(chip < last - 1)
    own_down = both(chip > 1)
    slot_of_row = lax.broadcasted_iota(jnp.int32, (slots * width, aux), 0) // width
    for m in range(row_blocks):
        product = jnp.dot(
            raw[m].reshape(slots * width, aux), metric[...], preferred_element_type=jnp.float32
        )
        kept = jnp.where(slot_of_row < live[0, m], product, 0.0).astype(jnp.bfloat16)
        for half in range(2):
            xs[core, chip, half, m] = kept[:, half * part : (half + 1) * part]

        if m == 0:
            pl.semaphore_wait(
                barrier, 2 * chips + groups - 2 + jnp.where(chip != grp, chips - 1, 0)
            )
            lax.fori_loop(0, 2 * chips, send_ids, 0)
            ids_vec[blk] = sig_vec[...]

        for cut in range(CUTS):
            @pl.when(own_up)
            def _():
                chain_copy(chip, LOW, m, cut, chip + 1).start()

            @pl.when(own_down)
            def _():
                chain_copy(chip, HIGH, m, cut, chip - 1).start()

    for half in range(2):
        for m in range(row_blocks):
            share_copy(core, chip, half, m).start()

    def lay_out():
        for half in range(2):
            for s in range(slots):
                block = jnp.concatenate(
                    [
                        xs[core, chip, half, m, s * width : (s + 1) * width, :]
                        for m in range(row_blocks)
                    ],
                    axis=0,
                )
                own[half, s] = block.astype(jnp.float32).T.astype(jnp.bfloat16)
            own[half, slots] = jnp.zeros((part, rows), jnp.bfloat16)

        row_block_of = lax.broadcasted_iota(jnp.int32, (part, rows), 1) // width
        for n in range(NOB_DEV):
            places = []
            for m in range(row_blocks):
                at = jnp.int32(slots)
                for s in range(slots):
                    at = jnp.where(sig_own[m, s] == n, s, at)
                places.append(at)
            for half in range(2):
                chosen = own[half, places[0]]
                for m in range(1, row_blocks):
                    chosen = jnp.where(row_block_of == m, own[half, places[m]], chosen)
                dense[half, n] = chosen

        acc[...] = jnp.zeros_like(acc)

    def add_products(from_core, source, half, m):
        block = jnp.concatenate(
            [xs[from_core, source, half, m, s * width : (s + 1) * width, :] for s in range(slots)],
            axis=1,
        )
        chosen = jnp.concatenate(
            [dense[half, ids[source * 2 + from_core, m, s]] for s in range(slots)], axis=0
        )
        here = pl.ds(pl.multiple_of(from_core * rows + m * width, width), width)
        acc[source, here, :] += jnp.dot(block, chosen, preferred_element_type=jnp.float32)

    def send_partial(source):
        def to_group(other, carry):
            @pl.when(other != grp)
            def _():
                red_copy(source, grp, other).start()
            return carry

        lax.fori_loop(0, groups, to_group, 0)

    def finish(source):
        def add_group(other, total):
            red_copy(source, other, other).wait_recv()
            return total + red[source, other]

        total = lax.fori_loop(0, grp, add_group, acc[source, rows_of(grp), :])
        half_sum[source] = lax.fori_loop(grp + 1, groups, add_group, total)

        @pl.when(source != chip)
        def _():
            swap_copy(source, core, lax.rem(grp, per_core)).start()

        @pl.when(source != grp)
        def _():
            keep_copy(source, grp).start()

        @pl.when(source == grp)
        def _():
            kept_sum[rows_of(grp), :] = half_sum[source]

    def send_other_half(m):
        for end, first, second, to_chip in ((0, LOW, HIGH, 1), (last, HIGH, LOW, last - 1)):
            @pl.when(chip == end)
            def _():
                for cut in range(CUTS):
                    chain_copy(chip, first, m, cut, to_chip).wait_send()
                    chain_copy(chip, second, m, cut, to_chip).start()

    def arrive(source, half, m, cut, onward, to_chip):
        chain_copy(source, half, m, cut, chip).wait_recv()

        if onward is not None:
            @pl.when(onward)
            def _():
                chain_copy(source, half, m, cut, to_chip).start()

        @pl.when(cut == CUTS - 1)
        def _():
            share_copy(core, source, half, m).start()

    def use(source, half, m):
        add_products(core, source, half, m)
        share_copy(sibling, source, half, m).wait_recv()
        add_products(sibling, source, half, m)

    def routes(step):
        below, above = chip - step, chip + step
        return (
            (up_valid(below), below, LOW, both(chip < last), chip + 1),
            (down_valid(above), above, HIGH, both(chip > 0), chip - 1),
            (both(step == 2, chip == 1), 0, HIGH, None, None),
            (both(step == 2, chip == last - 1), last, LOW, None, None),
        )

    def place_of(turn):
        whole = lax.div(turn, CUTS)
        return lax.div(whole, row_blocks) + 1, lax.rem(whole, row_blocks), lax.rem(turn, CUTS)

    def take_in(turn):
        step, m, cut = place_of(turn)
        for valid, source, half, onward, to_chip in routes(step):
            @pl.when(valid)
            def _():
                arrive(source, half, m, cut, onward, to_chip)

    def multiply(turn):
        step, m, cut = place_of(turn)
        for index, (valid, source, half, onward, to_chip) in enumerate(routes(step)):
            now = both(valid, cut == (0, CUTS - 1)[index % 2])

            @pl.when(now)
            def _():
                use(source, half, m)

            whole = both(now, m == row_blocks - 1)
            if index < 2:
                from_end = both(step == 1, source == (0, last)[index])
                whole = both(whole, jnp.logical_not(from_end))

            @pl.when(whole)
            def _():
                send_partial(source)

    def finish_distance(step):
        @pl.when(step == 0)
        def _():
            finish(chip)

        below, above = chip - step, chip + step
        from_ends = (both(step == 2, chip == 1), both(step == 2, chip == last - 1))
        for valid, source, end, from_end in (
            (up_valid(below), below, 0, from_ends[0]), (down_valid(above), above, last, from_ends[1])
        ):
            late = both(step == 1, source == end)

            @pl.when(both(valid, step > 0, jnp.logical_not(late)))
            def _():
                finish(source)

            @pl.when(from_end)
            def _():
                finish(end)

    turns = (chips - 1) * row_blocks * CUTS

    def one_turn(turn, carry):
        @pl.when(turn < turns)
        def _():
            take_in(turn)

        @pl.when(turn == 0)
        def _():
            lay_out()
            send_other_half(0)

        @pl.when(turn == 1)
        def _():
            @functools.partial(lax.fori_loop, 0, 2 * chips, init_val=0)
            def _(other, carry):
                @pl.when(other != blk)
                def _():
                    id_copy(other, other).wait_recv()
                return carry

            to_scalar = pltpu.make_async_copy(ids_vec, ids, id_local)
            to_scalar.start()
            to_scalar.wait()
            for half in range(2):
                for m in range(row_blocks):
                    add_products(core, chip, half, m)
            for m in range(1, row_blocks):
                send_other_half(m)

        @pl.when(turn == 2)
        def _():
            for half in range(2):
                for m in range(row_blocks):
                    share_copy(sibling, chip, half, m).wait_recv()
                    add_products(sibling, chip, half, m)
            send_partial(chip)

        @pl.when(turn > 2)
        def _():
            multiply(turn - 3)

        return carry

    lax.fori_loop(0, turns + 3, one_turn, 0)

    @functools.partial(lax.fori_loop, 0, chips, init_val=0)
    def _(step, carry):
        finish_distance(step)
        return carry

    mine = contributes(chip, grp)
    theirs = both(chip != grp, contributes(grp, chip))

    @pl.when(mine)
    def _():
        def wait_kept(other, carry):
            @pl.when(other != grp)
            def _():
                keep_copy(other, other).wait_recv()
            return carry

        lax.fori_loop(0, groups, wait_kept, 0)
        for core_at in range(2):
            here = slice(core_at * rows, (core_at + 1) * rows)
            out[:, here] = 0.25 * kept_sum[here, :].T

    @pl.when(theirs)
    def _():
        for core_at in range(2):
            for slot in range(per_core):
                swap_copy(chip, core_at, slot).wait_recv()

    @pl.when(both(mine, theirs))
    def _():
        for core_at in range(2):
            out[:, core_at * rows : (core_at + 1) * rows] += 0.25 * swap[core_at]

    @pl.when(jnp.logical_not(mine))
    def _():
        for core_at in range(2):
            out[:, core_at * rows : (core_at + 1) * rows] = 0.25 * swap[core_at]

    def done_ids(other, carry):
        @pl.when(other != blk)
        def _():
            id_copy(blk, other).wait_send()
        return carry

    lax.fori_loop(0, 2 * chips, done_ids, 0)

    def done_source(source, carry):
        low_here = jnp.logical_or(
            source == chip,
            jnp.logical_or(
                both(source < chip, contributes(chip, source)),
                both(source == last, chip == last - 1),
            ),
        )
        high_here = jnp.logical_or(
            source == chip,
            jnp.logical_or(
                both(source > chip, contributes(chip, source)),
                both(source == 0, chip == 1),
            ),
        )
        low_sent = jnp.logical_or(
            jnp.where(source == chip, both(own_up, chip > 0), both(source < chip, chip < last)),
            both(source == chip, chip == last),
        )
        high_sent = jnp.logical_or(
            jnp.where(source == chip, both(own_down, chip < last), both(source > chip, chip > 0)),
            both(source == chip, chip == 0),
        )
        for half, here, sent in ((LOW, low_here, low_sent), (HIGH, high_here, high_sent)):
            @pl.when(here)
            def _():
                for m in range(row_blocks):
                    share_copy(core, source, half, m).wait_send()

            @pl.when(sent)
            def _():
                for m in range(row_blocks):
                    for cut in range(CUTS):
                        chain_copy(source, half, m, cut, chip).wait_send()

        @pl.when(contributes(chip, source))
        def _():
            def done_group(other, inner):
                @pl.when(other != grp)
                def _():
                    red_copy(source, grp, other).wait_send()
                return inner

            lax.fori_loop(0, groups, done_group, 0)

            @pl.when(source != chip)
            def _():
                swap_copy(source, core, 0).wait_send()

            @pl.when(source != grp)
            def _():
                keep_copy(source, grp).wait_send()

        return carry

    lax.fori_loop(0, chips, done_source, 0)


def exchange_kernel(raw_blocks, metric_factor, sig_list, live_count):
    row_blocks, slots, width, aux = raw_blocks.shape
    blks, groups = lax.axis_size("blk"), lax.axis_size("grp")
    chips = blks // 2
    rows, part = row_blocks * width, aux // 2
    share = 2 * rows // groups
    vmem = pl.BlockSpec(memory_space=pltpu.VMEM)
    hbm = pl.BlockSpec(memory_space=pltpu.HBM)
    smem = pl.BlockSpec(memory_space=pltpu.SMEM)
    dma = pltpu.SemaphoreType.DMA
    return pl.pallas_call(
        functools.partial(kernel, chips, groups),
        out_shape=jax.ShapeDtypeStruct((rows, 2 * rows), jnp.float32),
        in_specs=[hbm, hbm, hbm, smem],
        out_specs=vmem,
        scratch_shapes=[
            pltpu.VMEM(raw_blocks.shape, jnp.bfloat16),
            pltpu.VMEM(metric_factor.shape, jnp.bfloat16),
            pltpu.VMEM(sig_list.shape, jnp.int32),
            pltpu.SMEM(sig_list.shape, jnp.int32),
            pltpu.VMEM((2, chips, 2, row_blocks, slots * width, part), jnp.bfloat16),
            pltpu.VMEM((2, slots + 1, part, rows), jnp.bfloat16),
            pltpu.VMEM((2, NOB_DEV, part, rows), jnp.bfloat16),
            pltpu.VMEM((blks, row_blocks, slots), jnp.int32),
            pltpu.SMEM((blks, row_blocks, slots), jnp.int32),
            pltpu.VMEM((chips, 2 * rows, rows), jnp.float32),
            pltpu.VMEM((chips, groups, share, rows), jnp.float32),
            pltpu.VMEM((chips, share, rows), jnp.float32),
            pltpu.VMEM((2 * rows, rows), jnp.float32),
            pltpu.VMEM((2, rows, rows), jnp.float32),
            dma((4,)), dma((blks,)), dma((blks,)), dma,
            dma((chips, 2, row_blocks, CUTS)), dma((chips, 2, row_blocks, CUTS)),
            dma((chips, 2, row_blocks)), dma((chips, 2, row_blocks)),
            dma((chips, groups)), dma((chips, groups)), dma((chips,)), dma((groups,)),
            dma((chips,)), dma((2, groups // 2)),
        ],
        compiler_params=pltpu.CompilerParams(
            collective_id=0, has_side_effects=True, vmem_limit_bytes=56400000
        ),
        cost_estimate=pl.CostEstimate(
            flops=2 * rows * 2 * rows * chips * slots * aux, bytes_accessed=2**20, transcendentals=0
        ),
    )(raw_blocks, metric_factor, sig_list, live_count.T)


def solution(mesh):
    placed = (P("blk", "grp", None, None), P(), P("blk", "grp"), P("blk", "grp"))
    return jax.shard_map(
        exchange_kernel, mesh=mesh, in_specs=placed, out_specs=P("blk", "grp"), check_vma=False
    )
```

```python
import functools

import jax
import jax.numpy as jnp
from jax import lax
from jax.experimental import pallas as pl
from jax.experimental.pallas import tpu as pltpu
from jax.sharding import PartitionSpec as P

NOB_DEV = 16
MESH = pl.DeviceIdType.MESH
CUTS = 3
LOW, HIGH = 0, 1


def both(*conditions):
    return functools.reduce(jnp.logical_and, conditions)


def kernel(
    chips, groups, raw_hbm, metric_hbm, sig_hbm, live, out,
    raw, metric, sig_vec, sig_own, xs, own, dense, ids_vec, ids, acc, red, half_sum, kept_sum, swap,
    in_sem, id_send, id_recv, id_local, chain_send, chain_recv, share_send, share_recv,
    red_send, red_recv, keep_send, keep_recv, swap_send, swap_recv,
):
    row_blocks, slots, width, aux = raw_hbm.shape
    part = aux // 2
    rows = row_blocks * width
    cut_rows = slots * width // CUTS
    blk, grp = lax.axis_index("blk"), lax.axis_index("grp")
    chip, core = lax.div(blk, 2), lax.rem(blk, 2)
    sibling = 1 - core
    last = chips - 1

    def contributes(at, to):
        return jnp.logical_not(
            jnp.logical_or(both(at == 0, to == 1), both(at == last, to == last - 1))
        )

    def up_valid(source):
        return both(source >= 0, contributes(chip, source))

    def down_valid(source):
        return both(source <= last, contributes(chip, source))

    def chain_copy(source, half, m, cut, to_chip):
        piece = xs.at[core, source, half, m, pl.ds(cut * cut_rows, cut_rows)]
        return pltpu.make_async_remote_copy(
            src_ref=piece, dst_ref=piece,
            send_sem=chain_send.at[source, half, m, cut],
            recv_sem=chain_recv.at[source, half, m, cut],
            device_id={"blk": to_chip * 2 + core, "grp": grp}, device_id_type=MESH,
        )

    def share_copy(from_core, source, half, m):
        piece = xs.at[from_core, source, half, m]
        return pltpu.make_async_remote_copy(
            src_ref=piece, dst_ref=piece,
            send_sem=share_send.at[source, half, m], recv_sem=share_recv.at[source, half, m],
            device_id={"blk": chip * 2 + sibling, "grp": grp}, device_id_type=MESH,
        )

    def id_copy(slot, to_blk):
        return pltpu.make_async_remote_copy(
            src_ref=sig_vec, dst_ref=ids_vec.at[slot],
            send_sem=id_send.at[to_blk], recv_sem=id_recv.at[slot],
            device_id={"blk": to_blk, "grp": grp}, device_id_type=MESH,
        )

    share = 2 * rows // groups
    per_core = groups // 2

    def rows_of(group):
        return pl.ds(pl.multiple_of(group * share, share), share)

    def red_copy(source, slot, to_grp):
        return pltpu.make_async_remote_copy(
            src_ref=acc.at[source, rows_of(to_grp)], dst_ref=red.at[source, slot],
            send_sem=red_send.at[source, to_grp], recv_sem=red_recv.at[source, slot],
            device_id={"blk": blk, "grp": to_grp}, device_id_type=MESH,
        )

    def keep_copy(source, slot):
        return pltpu.make_async_remote_copy(
            src_ref=half_sum.at[source], dst_ref=kept_sum.at[rows_of(slot)],
            send_sem=keep_send.at[source], recv_sem=keep_recv.at[slot],
            device_id={"blk": blk, "grp": source}, device_id_type=MESH,
        )

    def swap_copy(source, from_core, slot):
        return pltpu.make_async_remote_copy(
            src_ref=half_sum.at[source], dst_ref=swap.at[from_core, rows_of(slot)],
            send_sem=swap_send.at[source], recv_sem=swap_recv.at[from_core, slot],
            device_id={"blk": source * 2 + lax.div(grp, per_core), "grp": chip},
            device_id_type=MESH,
        )

    loads = [
        pltpu.make_async_copy(source, target, in_sem.at[index])
        for index, (source, target) in enumerate(
            ((raw_hbm, raw), (metric_hbm, metric), (sig_hbm, sig_vec), (sig_hbm, sig_own))
        )
    ]
    for load in loads:
        load.start()

    barrier = pltpu.get_barrier_semaphore()

    def greet_blk(other, carry):
        @pl.when(other != blk)
        def _():
            pl.semaphore_signal(
                barrier, inc=1, device_id={"blk": other, "grp": grp}, device_id_type=MESH
            )
        return carry

    def greet_grp(other, carry):
        @pl.when(other != grp)
        def _():
            pl.semaphore_signal(
                barrier, inc=1, device_id={"blk": blk, "grp": other}, device_id_type=MESH
            )
        return carry

    lax.fori_loop(0, 2 * chips, greet_blk, 0)
    lax.fori_loop(0, groups, greet_grp, 0)

    @pl.when(chip != grp)
    def _():
        for slot in range(per_core):
            group = core * per_core + slot

            @pl.when(group != grp)
            def _():
                for other in range(2):
                    pl.semaphore_signal(
                        barrier, inc=1, device_id={"blk": grp * 2 + other, "grp": group},
                        device_id_type=MESH,
                    )

    for load in loads:
        load.wait()

    def send_ids(other, carry):
        @pl.when(other != blk)
        def _():
            id_copy(blk, other).start()
        return carry

    own_up = both(chip < last - 1)
    own_down = both(chip > 1)
    slot_of_row = lax.broadcasted_iota(jnp.int32, (slots * width, aux), 0) // width
    for m in range(row_blocks):
        product = jnp.dot(
            raw[m].reshape(slots * width, aux), metric[...], preferred_element_type=jnp.float32
        )
        kept = jnp.where(slot_of_row < live[0, m], product, 0.0).astype(jnp.bfloat16)
        for half in range(2):
            xs[core, chip, half, m] = kept[:, half * part : (half + 1) * part]

        if m == 0:
            pl.semaphore_wait(
                barrier, 2 * chips + groups - 2 + jnp.where(chip != grp, chips - 1, 0)
            )
            lax.fori_loop(0, 2 * chips, send_ids, 0)
            ids_vec[blk] = sig_vec[...]

        for cut in range(CUTS):
            @pl.when(own_up)
            def _():
                chain_copy(chip, LOW, m, cut, chip + 1).start()

            @pl.when(own_down)
            def _():
                chain_copy(chip, HIGH, m, cut, chip - 1).start()

    for half in range(2):
        for m in range(row_blocks):
            share_copy(core, chip, half, m).start()

    def lay_out(half):
        for s in range(slots):
            block = jnp.concatenate(
                [
                    xs[core, chip, half, m, s * width : (s + 1) * width, :]
                    for m in range(row_blocks)
                ],
                axis=0,
            )
            own[half, s] = block.astype(jnp.float32).T.astype(jnp.bfloat16)
        own[half, slots] = jnp.zeros((part, rows), jnp.bfloat16)

        row_block_of = lax.broadcasted_iota(jnp.int32, (part, rows), 1) // width
        for n in range(NOB_DEV):
            places = []
            for m in range(row_blocks):
                at = jnp.int32(slots)
                for s in range(slots):
                    at = jnp.where(sig_own[m, s] == n, s, at)
                places.append(at)
            chosen = own[half, places[0]]
            for m in range(1, row_blocks):
                chosen = jnp.where(row_block_of == m, own[half, places[m]], chosen)
            dense[half, n] = chosen


    def add_products(from_core, source, half, m):
        block = jnp.concatenate(
            [xs[from_core, source, half, m, s * width : (s + 1) * width, :] for s in range(slots)],
            axis=1,
        )
        chosen = jnp.concatenate(
            [dense[half, ids[source * 2 + from_core, m, s]] for s in range(slots)], axis=0
        )
        here = pl.ds(pl.multiple_of(from_core * rows + m * width, width), width)
        acc[source, here, :] += jnp.dot(block, chosen, preferred_element_type=jnp.float32)

    def send_partial(source):
        def to_group(other, carry):
            @pl.when(other != grp)
            def _():
                red_copy(source, grp, other).start()
            return carry

        lax.fori_loop(0, groups, to_group, 0)

    def finish(source):
        def add_group(other, total):
            red_copy(source, other, other).wait_recv()
            return total + red[source, other]

        total = lax.fori_loop(0, grp, add_group, acc[source, rows_of(grp), :])
        half_sum[source] = lax.fori_loop(grp + 1, groups, add_group, total)

        @pl.when(source != chip)
        def _():
            swap_copy(source, core, lax.rem(grp, per_core)).start()

        @pl.when(source != grp)
        def _():
            keep_copy(source, grp).start()

        @pl.when(source == grp)
        def _():
            kept_sum[rows_of(grp), :] = half_sum[source]

    def send_other_half(m):
        for end, first, second, to_chip in ((0, LOW, HIGH, 1), (last, HIGH, LOW, last - 1)):
            @pl.when(chip == end)
            def _():
                for cut in range(CUTS):
                    chain_copy(chip, first, m, cut, to_chip).wait_send()
                    chain_copy(chip, second, m, cut, to_chip).start()

    def arrive(source, half, m, cut, onward, to_chip):
        chain_copy(source, half, m, cut, chip).wait_recv()

        if onward is not None:
            @pl.when(onward)
            def _():
                chain_copy(source, half, m, cut, to_chip).start()

        @pl.when(cut == CUTS - 1)
        def _():
            share_copy(core, source, half, m).start()

    def use(source, half, m):
        add_products(core, source, half, m)
        share_copy(sibling, source, half, m).wait_recv()
        add_products(sibling, source, half, m)

    def routes(step):
        below, above = chip - step, chip + step
        return (
            (up_valid(below), below, LOW, both(chip < last), chip + 1),
            (down_valid(above), above, HIGH, both(chip > 0), chip - 1),
            (both(step == 2, chip == 1), 0, HIGH, None, None),
            (both(step == 2, chip == last - 1), last, LOW, None, None),
        )

    def place_of(turn):
        whole = lax.div(turn, CUTS)
        return lax.div(whole, row_blocks) + 1, lax.rem(whole, row_blocks), lax.rem(turn, CUTS)

    def take_in(turn):
        step, m, cut = place_of(turn)
        for valid, source, half, onward, to_chip in routes(step):
            @pl.when(valid)
            def _():
                arrive(source, half, m, cut, onward, to_chip)

    def multiply(turn):
        step, m, cut = place_of(turn)
        for index, (valid, source, half, onward, to_chip) in enumerate(routes(step)):
            now = both(valid, cut == (0, CUTS - 1)[index % 2])

            @pl.when(now)
            def _():
                use(source, half, m)

            whole = both(now, m == row_blocks - 1)
            if index < 2:
                from_end = both(step == 1, source == (0, last)[index])
                whole = both(whole, jnp.logical_not(from_end))

            @pl.when(whole)
            def _():
                send_partial(source)

    def finish_distance(step):
        @pl.when(step == 0)
        def _():
            finish(chip)

        below, above = chip - step, chip + step
        from_ends = (both(step == 2, chip == 1), both(step == 2, chip == last - 1))
        for valid, source, end, from_end in (
            (up_valid(below), below, 0, from_ends[0]), (down_valid(above), above, last, from_ends[1])
        ):
            late = both(step == 1, source == end)

            @pl.when(both(valid, step > 0, jnp.logical_not(late)))
            def _():
                finish(source)

            @pl.when(from_end)
            def _():
                finish(end)

    turns = (chips - 1) * row_blocks * CUTS

    def one_turn(turn, carry):
        @pl.when(turn < turns)
        def _():
            take_in(turn)

        @pl.when(turn == 0)
        def _():
            lay_out(LOW)
            acc[...] = jnp.zeros_like(acc)

        @pl.when(turn == 1)
        def _():
            lay_out(HIGH)
            send_other_half(0)

        @pl.when(turn == 2)
        def _():
            @functools.partial(lax.fori_loop, 0, 2 * chips, init_val=0)
            def _(other, carry):
                @pl.when(other != blk)
                def _():
                    id_copy(other, other).wait_recv()
                return carry

            to_scalar = pltpu.make_async_copy(ids_vec, ids, id_local)
            to_scalar.start()
            to_scalar.wait()
            for half in range(2):
                for m in range(row_blocks):
                    add_products(core, chip, half, m)
            for m in range(1, row_blocks):
                send_other_half(m)

        @pl.when(turn == 3)
        def _():
            for half in range(2):
                for m in range(row_blocks):
                    share_copy(sibling, chip, half, m).wait_recv()
                    add_products(sibling, chip, half, m)
            send_partial(chip)

        @pl.when(turn > 3)
        def _():
            multiply(turn - 4)

        return carry

    lax.fori_loop(0, turns + 4, one_turn, 0)

    @functools.partial(lax.fori_loop, 0, chips, init_val=0)
    def _(step, carry):
        finish_distance(step)
        return carry

    mine = contributes(chip, grp)
    theirs = both(chip != grp, contributes(grp, chip))

    @pl.when(mine)
    def _():
        def wait_kept(other, carry):
            @pl.when(other != grp)
            def _():
                keep_copy(other, other).wait_recv()
            return carry

        lax.fori_loop(0, groups, wait_kept, 0)
        for core_at in range(2):
            here = slice(core_at * rows, (core_at + 1) * rows)
            out[:, here] = 0.25 * kept_sum[here, :].T

    @pl.when(theirs)
    def _():
        for core_at in range(2):
            for slot in range(per_core):
                swap_copy(chip, core_at, slot).wait_recv()

    @pl.when(both(mine, theirs))
    def _():
        for core_at in range(2):
            out[:, core_at * rows : (core_at + 1) * rows] += 0.25 * swap[core_at]

    @pl.when(jnp.logical_not(mine))
    def _():
        for core_at in range(2):
            out[:, core_at * rows : (core_at + 1) * rows] = 0.25 * swap[core_at]

    def done_ids(other, carry):
        @pl.when(other != blk)
        def _():
            id_copy(blk, other).wait_send()
        return carry

    lax.fori_loop(0, 2 * chips, done_ids, 0)

    def done_source(source, carry):
        low_here = jnp.logical_or(
            source == chip,
            jnp.logical_or(
                both(source < chip, contributes(chip, source)),
                both(source == last, chip == last - 1),
            ),
        )
        high_here = jnp.logical_or(
            source == chip,
            jnp.logical_or(
                both(source > chip, contributes(chip, source)),
                both(source == 0, chip == 1),
            ),
        )
        low_sent = jnp.logical_or(
            jnp.where(source == chip, both(own_up, chip > 0), both(source < chip, chip < last)),
            both(source == chip, chip == last),
        )
        high_sent = jnp.logical_or(
            jnp.where(source == chip, both(own_down, chip < last), both(source > chip, chip > 0)),
            both(source == chip, chip == 0),
        )
        for half, here, sent in ((LOW, low_here, low_sent), (HIGH, high_here, high_sent)):
            @pl.when(here)
            def _():
                for m in range(row_blocks):
                    share_copy(core, source, half, m).wait_send()

            @pl.when(sent)
            def _():
                for m in range(row_blocks):
                    for cut in range(CUTS):
                        chain_copy(source, half, m, cut, chip).wait_send()

        @pl.when(contributes(chip, source))
        def _():
            def done_group(other, inner):
                @pl.when(other != grp)
                def _():
                    red_copy(source, grp, other).wait_send()
                return inner

            lax.fori_loop(0, groups, done_group, 0)

            @pl.when(source != chip)
            def _():
                swap_copy(source, core, 0).wait_send()

            @pl.when(source != grp)
            def _():
                keep_copy(source, grp).wait_send()

        return carry

    lax.fori_loop(0, chips, done_source, 0)


def exchange_kernel(raw_blocks, metric_factor, sig_list, live_count):
    row_blocks, slots, width, aux = raw_blocks.shape
    blks, groups = lax.axis_size("blk"), lax.axis_size("grp")
    chips = blks // 2
    rows, part = row_blocks * width, aux // 2
    share = 2 * rows // groups
    vmem = pl.BlockSpec(memory_space=pltpu.VMEM)
    hbm = pl.BlockSpec(memory_space=pltpu.HBM)
    smem = pl.BlockSpec(memory_space=pltpu.SMEM)
    dma = pltpu.SemaphoreType.DMA
    return pl.pallas_call(
        functools.partial(kernel, chips, groups),
        out_shape=jax.ShapeDtypeStruct((rows, 2 * rows), jnp.float32),
        in_specs=[hbm, hbm, hbm, smem],
        out_specs=vmem,
        scratch_shapes=[
            pltpu.VMEM(raw_blocks.shape, jnp.bfloat16),
            pltpu.VMEM(metric_factor.shape, jnp.bfloat16),
            pltpu.VMEM(sig_list.shape, jnp.int32),
            pltpu.SMEM(sig_list.shape, jnp.int32),
            pltpu.VMEM((2, chips, 2, row_blocks, slots * width, part), jnp.bfloat16),
            pltpu.VMEM((2, slots + 1, part, rows), jnp.bfloat16),
            pltpu.VMEM((2, NOB_DEV, part, rows), jnp.bfloat16),
            pltpu.VMEM((blks, row_blocks, slots), jnp.int32),
            pltpu.SMEM((blks, row_blocks, slots), jnp.int32),
            pltpu.VMEM((chips, 2 * rows, rows), jnp.float32),
            pltpu.VMEM((chips, groups, share, rows), jnp.float32),
            pltpu.VMEM((chips, share, rows), jnp.float32),
            pltpu.VMEM((2 * rows, rows), jnp.float32),
            pltpu.VMEM((2, rows, rows), jnp.float32),
            dma((4,)), dma((blks,)), dma((blks,)), dma,
            dma((chips, 2, row_blocks, CUTS)), dma((chips, 2, row_blocks, CUTS)),
            dma((chips, 2, row_blocks)), dma((chips, 2, row_blocks)),
            dma((chips, groups)), dma((chips, groups)), dma((chips,)), dma((groups,)),
            dma((chips,)), dma((2, groups // 2)),
        ],
        compiler_params=pltpu.CompilerParams(
            collective_id=0, has_side_effects=True, vmem_limit_bytes=56400000
        ),
        cost_estimate=pl.CostEstimate(
            flops=2 * rows * 2 * rows * chips * slots * aux, bytes_accessed=2**20, transcendentals=0
        ),
    )(raw_blocks, metric_factor, sig_list, live_count.T)


def solution(mesh):
    placed = (P("blk", "grp", None, None), P(), P("blk", "grp"), P("blk", "grp"))
    return jax.shard_map(
        exchange_kernel, mesh=mesh, in_specs=placed, out_specs=P("blk", "grp"), check_vma=False
    )
```

```python
import functools

import jax
import jax.numpy as jnp
from jax import lax
from jax.experimental import pallas as pl
from jax.experimental.pallas import tpu as pltpu
from jax.sharding import PartitionSpec as P

NOB_DEV = 16
MESH = pl.DeviceIdType.MESH
CUTS = 2
LOW, HIGH = 0, 1


def both(*conditions):
    return functools.reduce(jnp.logical_and, conditions)


def kernel(
    chips, groups, raw_hbm, metric_hbm, sig_hbm, live, out,
    raw, metric, sig_vec, sig_own, xs, own, dense, ids_vec, ids, acc, red, half_sum, kept_sum, swap,
    in_sem, id_send, id_recv, id_local, chain_send, chain_recv, share_send, share_recv,
    red_send, red_recv, keep_send, keep_recv, swap_send, swap_recv,
):
    row_blocks, slots, width, aux = raw_hbm.shape
    part = aux // 2
    rows = row_blocks * width
    cut_rows = slots * width // CUTS
    blk, grp = lax.axis_index("blk"), lax.axis_index("grp")
    chip, core = lax.div(blk, 2), lax.rem(blk, 2)
    sibling = 1 - core
    last = chips - 1

    def contributes(at, to):
        return jnp.logical_not(
            jnp.logical_or(both(at == 0, to == 1), both(at == last, to == last - 1))
        )

    def up_valid(source):
        return both(source >= 0, contributes(chip, source))

    def down_valid(source):
        return both(source <= last, contributes(chip, source))

    def chain_copy(source, half, m, cut, to_chip):
        piece = xs.at[core, source, half, m, pl.ds(cut * cut_rows, cut_rows)]
        return pltpu.make_async_remote_copy(
            src_ref=piece, dst_ref=piece,
            send_sem=chain_send.at[source, half, m, cut],
            recv_sem=chain_recv.at[source, half, m, cut],
            device_id={"blk": to_chip * 2 + core, "grp": grp}, device_id_type=MESH,
        )

    def share_copy(from_core, source, half, m):
        piece = xs.at[from_core, source, half, m]
        return pltpu.make_async_remote_copy(
            src_ref=piece, dst_ref=piece,
            send_sem=share_send.at[source, half, m], recv_sem=share_recv.at[source, half, m],
            device_id={"blk": chip * 2 + sibling, "grp": grp}, device_id_type=MESH,
        )

    def id_copy(slot, to_blk):
        return pltpu.make_async_remote_copy(
            src_ref=sig_vec, dst_ref=ids_vec.at[slot],
            send_sem=id_send.at[to_blk], recv_sem=id_recv.at[slot],
            device_id={"blk": to_blk, "grp": grp}, device_id_type=MESH,
        )

    share = 2 * rows // groups
    per_core = groups // 2

    def rows_of(group):
        return pl.ds(pl.multiple_of(group * share, share), share)

    def red_copy(source, slot, to_grp):
        return pltpu.make_async_remote_copy(
            src_ref=acc.at[source, rows_of(to_grp)], dst_ref=red.at[source, slot],
            send_sem=red_send.at[source, to_grp], recv_sem=red_recv.at[source, slot],
            device_id={"blk": blk, "grp": to_grp}, device_id_type=MESH,
        )

    def keep_copy(source, slot):
        return pltpu.make_async_remote_copy(
            src_ref=half_sum.at[source], dst_ref=kept_sum.at[rows_of(slot)],
            send_sem=keep_send.at[source], recv_sem=keep_recv.at[slot],
            device_id={"blk": blk, "grp": source}, device_id_type=MESH,
        )

    def swap_copy(source, from_core, slot):
        return pltpu.make_async_remote_copy(
            src_ref=half_sum.at[source], dst_ref=swap.at[from_core, rows_of(slot)],
            send_sem=swap_send.at[source], recv_sem=swap_recv.at[from_core, slot],
            device_id={"blk": source * 2 + lax.div(grp, per_core), "grp": chip},
            device_id_type=MESH,
        )

    loads = [
        pltpu.make_async_copy(source, target, in_sem.at[index])
        for index, (source, target) in enumerate(
            ((raw_hbm, raw), (metric_hbm, metric), (sig_hbm, sig_vec), (sig_hbm, sig_own))
        )
    ]
    for load in loads:
        load.start()

    barrier = pltpu.get_barrier_semaphore()

    def greet_blk(other, carry):
        @pl.when(other != blk)
        def _():
            pl.semaphore_signal(
                barrier, inc=1, device_id={"blk": other, "grp": grp}, device_id_type=MESH
            )
        return carry

    def greet_grp(other, carry):
        @pl.when(other != grp)
        def _():
            pl.semaphore_signal(
                barrier, inc=1, device_id={"blk": blk, "grp": other}, device_id_type=MESH
            )
        return carry

    lax.fori_loop(0, 2 * chips, greet_blk, 0)
    lax.fori_loop(0, groups, greet_grp, 0)

    @pl.when(chip != grp)
    def _():
        for slot in range(per_core):
            group = core * per_core + slot

            @pl.when(group != grp)
            def _():
                for other in range(2):
                    pl.semaphore_signal(
                        barrier, inc=1, device_id={"blk": grp * 2 + other, "grp": group},
                        device_id_type=MESH,
                    )

    for load in loads:
        load.wait()

    def send_ids(other, carry):
        @pl.when(other != blk)
        def _():
            id_copy(blk, other).start()
        return carry

    own_up = both(chip < last - 1)
    own_down = both(chip > 1)
    slot_of_row = lax.broadcasted_iota(jnp.int32, (slots * width, aux), 0) // width
    for m in range(row_blocks):
        product = jnp.dot(
            raw[m].reshape(slots * width, aux), metric[...], preferred_element_type=jnp.float32
        )
        kept = jnp.where(slot_of_row < live[0, m], product, 0.0).astype(jnp.bfloat16)
        for half in range(2):
            xs[core, chip, half, m] = kept[:, half * part : (half + 1) * part]

        if m == 0:
            pl.semaphore_wait(
                barrier, 2 * chips + groups - 2 + jnp.where(chip != grp, chips - 1, 0)
            )
            lax.fori_loop(0, 2 * chips, send_ids, 0)
            ids_vec[blk] = sig_vec[...]

        for cut in range(CUTS):
            @pl.when(own_up)
            def _():
                chain_copy(chip, LOW, m, cut, chip + 1).start()

            @pl.when(own_down)
            def _():
                chain_copy(chip, HIGH, m, cut, chip - 1).start()

    for half in range(2):
        for m in range(row_blocks):
            share_copy(core, chip, half, m).start()

    def lay_out():
        for half in range(2):
            for s in range(slots):
                block = jnp.concatenate(
                    [
                        xs[core, chip, half, m, s * width : (s + 1) * width, :]
                        for m in range(row_blocks)
                    ],
                    axis=0,
                )
                own[half, s] = block.astype(jnp.float32).T.astype(jnp.bfloat16)
            own[half, slots] = jnp.zeros((part, rows), jnp.bfloat16)

        row_block_of = lax.broadcasted_iota(jnp.int32, (part, rows), 1) // width
        for n in range(NOB_DEV):
            places = []
            for m in range(row_blocks):
                at = jnp.int32(slots)
                for s in range(slots):
                    at = jnp.where(sig_own[m, s] == n, s, at)
                places.append(at)
            for half in range(2):
                chosen = own[half, places[0]]
                for m in range(1, row_blocks):
                    chosen = jnp.where(row_block_of == m, own[half, places[m]], chosen)
                dense[half, n] = chosen

        acc[...] = jnp.zeros_like(acc)

    def add_products(from_core, source, half, m):
        block = jnp.concatenate(
            [xs[from_core, source, half, m, s * width : (s + 1) * width, :] for s in range(slots)],
            axis=1,
        )
        chosen = jnp.concatenate(
            [dense[half, ids[source * 2 + from_core, m, s]] for s in range(slots)], axis=0
        )
        here = pl.ds(pl.multiple_of(from_core * rows + m * width, width), width)
        acc[source, here, :] += jnp.dot(block, chosen, preferred_element_type=jnp.float32)

    per_block = per_core // row_blocks

    def send_partial(source, m):
        for core_at in range(2):
            for place in range(per_block):
                other = core_at * per_core + m * per_block + place

                @pl.when(other != grp)
                def _():
                    red_copy(source, grp, other).start()

    def finish(source):
        def add_group(other, total):
            red_copy(source, other, other).wait_recv()
            return total + red[source, other]

        total = lax.fori_loop(0, grp, add_group, acc[source, rows_of(grp), :])
        half_sum[source] = lax.fori_loop(grp + 1, groups, add_group, total)

        @pl.when(source != chip)
        def _():
            swap_copy(source, core, lax.rem(grp, per_core)).start()

        @pl.when(source != grp)
        def _():
            keep_copy(source, grp).start()

        @pl.when(source == grp)
        def _():
            kept_sum[rows_of(grp), :] = half_sum[source]

    def send_other_half(m):
        for end, first, second, to_chip in ((0, LOW, HIGH, 1), (last, HIGH, LOW, last - 1)):
            @pl.when(chip == end)
            def _():
                for cut in range(CUTS):
                    chain_copy(chip, first, m, cut, to_chip).wait_send()
                    chain_copy(chip, second, m, cut, to_chip).start()

    def arrive(source, half, m, cut, onward, to_chip):
        chain_copy(source, half, m, cut, chip).wait_recv()

        if onward is not None:
            @pl.when(onward)
            def _():
                chain_copy(source, half, m, cut, to_chip).start()

        @pl.when(cut == CUTS - 1)
        def _():
            share_copy(core, source, half, m).start()

    def use(source, half, m):
        add_products(core, source, half, m)
        share_copy(sibling, source, half, m).wait_recv()
        add_products(sibling, source, half, m)

    def routes(step):
        below, above = chip - step, chip + step
        return (
            (up_valid(below), below, LOW, both(chip < last), chip + 1),
            (down_valid(above), above, HIGH, both(chip > 0), chip - 1),
            (both(step == 2, chip == 1), 0, HIGH, None, None),
            (both(step == 2, chip == last - 1), last, LOW, None, None),
        )

    def place_of(turn):
        whole = lax.div(turn, CUTS)
        return lax.div(whole, row_blocks) + 1, lax.rem(whole, row_blocks), lax.rem(turn, CUTS)

    def take_in(turn):
        step, m, cut = place_of(turn)
        for valid, source, half, onward, to_chip in routes(step):
            @pl.when(valid)
            def _():
                arrive(source, half, m, cut, onward, to_chip)

    def multiply(turn):
        step, m, cut = place_of(turn)
        for index, (valid, source, half, onward, to_chip) in enumerate(routes(step)):
            now = both(valid, cut == (0, CUTS - 1)[index % 2])

            @pl.when(now)
            def _():
                use(source, half, m)

            whole = now
            if index < 2:
                from_end = both(step == 1, source == (0, last)[index])
                whole = both(whole, jnp.logical_not(from_end))

            @pl.when(whole)
            def _():
                send_partial(source, m)

    def finish_distance(step):
        @pl.when(step == 0)
        def _():
            finish(chip)

        below, above = chip - step, chip + step
        from_ends = (both(step == 2, chip == 1), both(step == 2, chip == last - 1))
        for valid, source, end, from_end in (
            (up_valid(below), below, 0, from_ends[0]), (down_valid(above), above, last, from_ends[1])
        ):
            late = both(step == 1, source == end)

            @pl.when(both(valid, step > 0, jnp.logical_not(late)))
            def _():
                finish(source)

            @pl.when(from_end)
            def _():
                finish(end)

    turns = (chips - 1) * row_blocks * CUTS

    def one_turn(turn, carry):
        @pl.when(turn < turns)
        def _():
            take_in(turn)

        @pl.when(turn == 0)
        def _():
            lay_out()
            send_other_half(0)

        @pl.when(turn == 1)
        def _():
            @functools.partial(lax.fori_loop, 0, 2 * chips, init_val=0)
            def _(other, carry):
                @pl.when(other != blk)
                def _():
                    id_copy(other, other).wait_recv()
                return carry

            to_scalar = pltpu.make_async_copy(ids_vec, ids, id_local)
            to_scalar.start()
            to_scalar.wait()
            for half in range(2):
                for m in range(row_blocks):
                    add_products(core, chip, half, m)
            for m in range(1, row_blocks):
                send_other_half(m)

        @pl.when(turn == 2)
        def _():
            for half in range(2):
                for m in range(row_blocks):
                    share_copy(sibling, chip, half, m).wait_recv()
                    add_products(sibling, chip, half, m)
            for m in range(row_blocks):
                send_partial(chip, m)

        @pl.when(turn > 2)
        def _():
            multiply(turn - 3)

        return carry

    lax.fori_loop(0, turns + 3, one_turn, 0)

    @functools.partial(lax.fori_loop, 0, chips, init_val=0)
    def _(step, carry):
        finish_distance(step)
        return carry

    def done_ids(other, carry):
        @pl.when(other != blk)
        def _():
            id_copy(blk, other).wait_send()
        return carry

    lax.fori_loop(0, 2 * chips, done_ids, 0)

    def done_source(source, carry):
        low_here = jnp.logical_or(
            source == chip,
            jnp.logical_or(
                both(source < chip, contributes(chip, source)),
                both(source == last, chip == last - 1),
            ),
        )
        high_here = jnp.logical_or(
            source == chip,
            jnp.logical_or(
                both(source > chip, contributes(chip, source)),
                both(source == 0, chip == 1),
            ),
        )
        low_sent = jnp.logical_or(
            jnp.where(source == chip, both(own_up, chip > 0), both(source < chip, chip < last)),
            both(source == chip, chip == last),
        )
        high_sent = jnp.logical_or(
            jnp.where(source == chip, both(own_down, chip < last), both(source > chip, chip > 0)),
            both(source == chip, chip == 0),
        )
        for half, here, sent in ((LOW, low_here, low_sent), (HIGH, high_here, high_sent)):
            @pl.when(here)
            def _():
                for m in range(row_blocks):
                    share_copy(core, source, half, m).wait_send()

            @pl.when(sent)
            def _():
                for m in range(row_blocks):
                    for cut in range(CUTS):
                        chain_copy(source, half, m, cut, chip).wait_send()

        @pl.when(contributes(chip, source))
        def _():
            def done_group(other, inner):
                @pl.when(other != grp)
                def _():
                    red_copy(source, grp, other).wait_send()
                return inner

            lax.fori_loop(0, groups, done_group, 0)

        return carry

    lax.fori_loop(0, chips, done_source, 0)

    mine = contributes(chip, grp)
    theirs = both(chip != grp, contributes(grp, chip))

    @pl.when(mine)
    def _():
        def wait_kept(other, carry):
            @pl.when(other != grp)
            def _():
                keep_copy(other, other).wait_recv()
            return carry

        lax.fori_loop(0, groups, wait_kept, 0)
        for core_at in range(2):
            here = slice(core_at * rows, (core_at + 1) * rows)
            out[:, here] = 0.25 * kept_sum[here, :].T

    @pl.when(theirs)
    def _():
        for core_at in range(2):
            for slot in range(per_core):
                swap_copy(chip, core_at, slot).wait_recv()

    @pl.when(both(mine, theirs))
    def _():
        for core_at in range(2):
            out[:, core_at * rows : (core_at + 1) * rows] += 0.25 * swap[core_at]

    @pl.when(jnp.logical_not(mine))
    def _():
        for core_at in range(2):
            out[:, core_at * rows : (core_at + 1) * rows] = 0.25 * swap[core_at]

    def done_sums(source, carry):
        @pl.when(contributes(chip, source))
        def _():
            @pl.when(source != chip)
            def _():
                swap_copy(source, core, 0).wait_send()

            @pl.when(source != grp)
            def _():
                keep_copy(source, grp).wait_send()

        return carry

    lax.fori_loop(0, chips, done_sums, 0)


def exchange_kernel(raw_blocks, metric_factor, sig_list, live_count):
    row_blocks, slots, width, aux = raw_blocks.shape
    blks, groups = lax.axis_size("blk"), lax.axis_size("grp")
    chips = blks // 2
    rows, part = row_blocks * width, aux // 2
    share = 2 * rows // groups
    vmem = pl.BlockSpec(memory_space=pltpu.VMEM)
    hbm = pl.BlockSpec(memory_space=pltpu.HBM)
    smem = pl.BlockSpec(memory_space=pltpu.SMEM)
    dma = pltpu.SemaphoreType.DMA
    return pl.pallas_call(
        functools.partial(kernel, chips, groups),
        out_shape=jax.ShapeDtypeStruct((rows, 2 * rows), jnp.float32),
        in_specs=[hbm, hbm, hbm, smem],
        out_specs=vmem,
        scratch_shapes=[
            pltpu.VMEM(raw_blocks.shape, jnp.bfloat16),
            pltpu.VMEM(metric_factor.shape, jnp.bfloat16),
            pltpu.VMEM(sig_list.shape, jnp.int32),
            pltpu.SMEM(sig_list.shape, jnp.int32),
            pltpu.VMEM((2, chips, 2, row_blocks, slots * width, part), jnp.bfloat16),
            pltpu.VMEM((2, slots + 1, part, rows), jnp.bfloat16),
            pltpu.VMEM((2, NOB_DEV, part, rows), jnp.bfloat16),
            pltpu.VMEM((blks, row_blocks, slots), jnp.int32),
            pltpu.SMEM((blks, row_blocks, slots), jnp.int32),
            pltpu.VMEM((chips, 2 * rows, rows), jnp.float32),
            pltpu.VMEM((chips, groups, share, rows), jnp.float32),
            pltpu.VMEM((chips, share, rows), jnp.float32),
            pltpu.VMEM((2 * rows, rows), jnp.float32),
            pltpu.VMEM((2, rows, rows), jnp.float32),
            dma((4,)), dma((blks,)), dma((blks,)), dma,
            dma((chips, 2, row_blocks, CUTS)), dma((chips, 2, row_blocks, CUTS)),
            dma((chips, 2, row_blocks)), dma((chips, 2, row_blocks)),
            dma((chips, groups)), dma((chips, groups)), dma((chips,)), dma((groups,)),
            dma((chips,)), dma((2, groups // 2)),
        ],
        compiler_params=pltpu.CompilerParams(
            collective_id=0, has_side_effects=True, vmem_limit_bytes=56400000
        ),
        cost_estimate=pl.CostEstimate(
            flops=2 * rows * 2 * rows * chips * slots * aux, bytes_accessed=2**20, transcendentals=0
        ),
    )(raw_blocks, metric_factor, sig_list, live_count.T)


def solution(mesh):
    placed = (P("blk", "grp", None, None), P(), P("blk", "grp"), P("blk", "grp"))
    return jax.shard_map(
        exchange_kernel, mesh=mesh, in_specs=placed, out_specs=P("blk", "grp"), check_vma=False
    )
```

```python
import functools

import jax
import jax.numpy as jnp
from jax import lax
from jax.experimental import pallas as pl
from jax.experimental.pallas import tpu as pltpu
from jax.sharding import PartitionSpec as P

NOB_DEV = 16
MESH = pl.DeviceIdType.MESH
CUTS = 2
LOW, HIGH = 0, 1


def both(*conditions):
    return functools.reduce(jnp.logical_and, conditions)


def kernel(
    chips, groups, raw_hbm, metric_hbm, sig_hbm, live, out,
    raw, metric, sig_vec, sig_own, xs, own, dense, ids_vec, ids, acc, red, half_sum, kept_sum, swap,
    in_sem, id_send, id_recv, id_local, chain_send, chain_recv, share_send, share_recv,
    red_send, red_recv, keep_send, keep_recv, swap_send, swap_recv,
):
    row_blocks, slots, width, aux = raw_hbm.shape
    part = aux // 2
    rows = row_blocks * width
    cut_rows = slots * width // CUTS
    blk, grp = lax.axis_index("blk"), lax.axis_index("grp")
    chip, core = lax.div(blk, 2), lax.rem(blk, 2)
    sibling = 1 - core
    last = chips - 1

    def contributes(at, to):
        return jnp.logical_not(
            jnp.logical_or(both(at == 0, to == 1), both(at == last, to == last - 1))
        )

    def up_valid(source):
        return both(source >= 0, contributes(chip, source))

    def down_valid(source):
        return both(source <= last, contributes(chip, source))

    def chain_copy(source, half, m, cut, to_chip):
        piece = xs.at[core, source, half, m, pl.ds(cut * cut_rows, cut_rows)]
        return pltpu.make_async_remote_copy(
            src_ref=piece, dst_ref=piece,
            send_sem=chain_send.at[source, half, m, cut],
            recv_sem=chain_recv.at[source, half, m, cut],
            device_id={"blk": to_chip * 2 + core, "grp": grp}, device_id_type=MESH,
        )

    def share_copy(from_core, source, half, m):
        piece = xs.at[from_core, source, half, m]
        return pltpu.make_async_remote_copy(
            src_ref=piece, dst_ref=piece,
            send_sem=share_send.at[source, half, m], recv_sem=share_recv.at[source, half, m],
            device_id={"blk": chip * 2 + sibling, "grp": grp}, device_id_type=MESH,
        )

    def id_copy(slot, to_blk):
        return pltpu.make_async_remote_copy(
            src_ref=sig_vec, dst_ref=ids_vec.at[slot],
            send_sem=id_send.at[to_blk], recv_sem=id_recv.at[slot],
            device_id={"blk": to_blk, "grp": grp}, device_id_type=MESH,
        )

    share = 2 * rows // groups
    per_core = groups // 2

    def rows_of(group):
        return pl.ds(pl.multiple_of(group * share, share), share)

    def red_copy(source, slot, to_grp):
        return pltpu.make_async_remote_copy(
            src_ref=acc.at[source, rows_of(to_grp)], dst_ref=red.at[source, slot],
            send_sem=red_send.at[source, to_grp], recv_sem=red_recv.at[source, slot],
            device_id={"blk": blk, "grp": to_grp}, device_id_type=MESH,
        )

    def keep_copy(source, slot):
        return pltpu.make_async_remote_copy(
            src_ref=half_sum.at[source], dst_ref=kept_sum.at[rows_of(slot)],
            send_sem=keep_send.at[source], recv_sem=keep_recv.at[slot],
            device_id={"blk": blk, "grp": source}, device_id_type=MESH,
        )

    def swap_copy(source, from_core, slot):
        return pltpu.make_async_remote_copy(
            src_ref=half_sum.at[source], dst_ref=swap.at[from_core, rows_of(slot)],
            send_sem=swap_send.at[source], recv_sem=swap_recv.at[from_core, slot],
            device_id={"blk": source * 2 + lax.div(grp, per_core), "grp": chip},
            device_id_type=MESH,
        )

    loads = [
        pltpu.make_async_copy(source, target, in_sem.at[index])
        for index, (source, target) in enumerate(
            ((raw_hbm, raw), (metric_hbm, metric), (sig_hbm, sig_vec), (sig_hbm, sig_own))
        )
    ]
    for load in loads:
        load.start()

    barrier = pltpu.get_barrier_semaphore()

    def greet_blk(other, carry):
        @pl.when(other != blk)
        def _():
            pl.semaphore_signal(
                barrier, inc=1, device_id={"blk": other, "grp": grp}, device_id_type=MESH
            )
        return carry

    def greet_grp(other, carry):
        @pl.when(other != grp)
        def _():
            pl.semaphore_signal(
                barrier, inc=1, device_id={"blk": blk, "grp": other}, device_id_type=MESH
            )
        return carry

    lax.fori_loop(0, 2 * chips, greet_blk, 0)
    lax.fori_loop(0, groups, greet_grp, 0)

    @pl.when(chip != grp)
    def _():
        for slot in range(per_core):
            group = core * per_core + slot

            @pl.when(group != grp)
            def _():
                for other in range(2):
                    pl.semaphore_signal(
                        barrier, inc=1, device_id={"blk": grp * 2 + other, "grp": group},
                        device_id_type=MESH,
                    )

    for load in loads:
        load.wait()

    def send_ids(other, carry):
        @pl.when(other != blk)
        def _():
            id_copy(blk, other).start()
        return carry

    own_up = both(chip < last - 1)
    own_down = both(chip > 1)
    slot_of_row = lax.broadcasted_iota(jnp.int32, (slots * width, aux), 0) // width
    for m in range(row_blocks):
        product = jnp.dot(
            raw[m].reshape(slots * width, aux), metric[...], preferred_element_type=jnp.float32
        )
        kept = jnp.where(slot_of_row < live[0, m], product, 0.0).astype(jnp.bfloat16)
        for half in range(2):
            xs[core, chip, half, m] = kept[:, half * part : (half + 1) * part]

        if m == 0:
            pl.semaphore_wait(
                barrier, 2 * chips + groups - 2 + jnp.where(chip != grp, chips - 1, 0)
            )
            lax.fori_loop(0, 2 * chips, send_ids, 0)
            ids_vec[blk] = sig_vec[...]

        for cut in range(CUTS):
            @pl.when(own_up)
            def _():
                chain_copy(chip, LOW, m, cut, chip + 1).start()

            @pl.when(own_down)
            def _():
                chain_copy(chip, HIGH, m, cut, chip - 1).start()

    for half in range(2):
        for m in range(row_blocks):
            share_copy(core, chip, half, m).start()

    def lay_out(half):
        for s in range(slots):
            block = jnp.concatenate(
                [
                    xs[core, chip, half, m, s * width : (s + 1) * width, :]
                    for m in range(row_blocks)
                ],
                axis=0,
            )
            own[half, s] = block.astype(jnp.float32).T.astype(jnp.bfloat16)
        own[half, slots] = jnp.zeros((part, rows), jnp.bfloat16)

        row_block_of = lax.broadcasted_iota(jnp.int32, (part, rows), 1) // width
        for n in range(NOB_DEV):
            places = []
            for m in range(row_blocks):
                at = jnp.int32(slots)
                for s in range(slots):
                    at = jnp.where(sig_own[m, s] == n, s, at)
                places.append(at)
            chosen = own[half, places[0]]
            for m in range(1, row_blocks):
                chosen = jnp.where(row_block_of == m, own[half, places[m]], chosen)
            dense[half, n] = chosen

    def add_products(from_core, source, half, m):
        block = jnp.concatenate(
            [xs[from_core, source, half, m, s * width : (s + 1) * width, :] for s in range(slots)],
            axis=1,
        )
        chosen = jnp.concatenate(
            [dense[half, ids[source * 2 + from_core, m, s]] for s in range(slots)], axis=0
        )
        here = pl.ds(pl.multiple_of(from_core * rows + m * width, width), width)
        acc[source, here, :] += jnp.dot(block, chosen, preferred_element_type=jnp.float32)

    per_block = per_core // row_blocks

    def send_partial(source, m):
        for core_at in range(2):
            for place in range(per_block):
                other = core_at * per_core + m * per_block + place

                @pl.when(other != grp)
                def _():
                    red_copy(source, grp, other).start()

    def finish(source):
        def add_group(other, total):
            red_copy(source, other, other).wait_recv()
            return total + red[source, other]

        total = lax.fori_loop(0, grp, add_group, acc[source, rows_of(grp), :])
        half_sum[source] = lax.fori_loop(grp + 1, groups, add_group, total)

        @pl.when(source != chip)
        def _():
            swap_copy(source, core, lax.rem(grp, per_core)).start()

        @pl.when(source != grp)
        def _():
            keep_copy(source, grp).start()

        @pl.when(source == grp)
        def _():
            kept_sum[rows_of(grp), :] = half_sum[source]

    def send_other_half(m):
        for end, first, second, to_chip in ((0, LOW, HIGH, 1), (last, HIGH, LOW, last - 1)):
            @pl.when(chip == end)
            def _():
                for cut in range(CUTS):
                    chain_copy(chip, first, m, cut, to_chip).wait_send()
                    chain_copy(chip, second, m, cut, to_chip).start()

    def arrive(source, half, m, cut, onward, to_chip):
        chain_copy(source, half, m, cut, chip).wait_recv()

        if onward is not None:
            @pl.when(onward)
            def _():
                chain_copy(source, half, m, cut, to_chip).start()

        @pl.when(cut == CUTS - 1)
        def _():
            share_copy(core, source, half, m).start()

    def use(source, half, m):
        add_products(core, source, half, m)
        share_copy(sibling, source, half, m).wait_recv()
        add_products(sibling, source, half, m)

    def routes(step):
        below, above = chip - step, chip + step
        return (
            (up_valid(below), below, LOW, both(chip < last), chip + 1),
            (down_valid(above), above, HIGH, both(chip > 0), chip - 1),
            (both(step == 2, chip == 1), 0, HIGH, None, None),
            (both(step == 2, chip == last - 1), last, LOW, None, None),
        )

    def place_of(turn):
        whole = lax.div(turn, CUTS)
        return lax.div(whole, row_blocks) + 1, lax.rem(whole, row_blocks), lax.rem(turn, CUTS)

    def take_in(turn):
        step, m, cut = place_of(turn)
        for valid, source, half, onward, to_chip in routes(step):
            @pl.when(valid)
            def _():
                arrive(source, half, m, cut, onward, to_chip)

    def multiply(turn):
        step, m, cut = place_of(turn)
        for index, (valid, source, half, onward, to_chip) in enumerate(routes(step)):
            now = both(valid, cut == (0, CUTS - 1)[index % 2])

            @pl.when(now)
            def _():
                use(source, half, m)

            whole = now
            if index < 2:
                from_end = both(step == 1, source == (0, last)[index])
                whole = both(whole, jnp.logical_not(from_end))

            @pl.when(whole)
            def _():
                send_partial(source, m)

    def finish_distance(step):
        @pl.when(step == 0)
        def _():
            finish(chip)

        below, above = chip - step, chip + step
        from_ends = (both(step == 2, chip == 1), both(step == 2, chip == last - 1))
        for valid, source, end, from_end in (
            (up_valid(below), below, 0, from_ends[0]), (down_valid(above), above, last, from_ends[1])
        ):
            late = both(step == 1, source == end)

            @pl.when(both(valid, step > 0, jnp.logical_not(late)))
            def _():
                finish(source)

            @pl.when(from_end)
            def _():
                finish(end)

    turns = (chips - 1) * row_blocks * CUTS

    def one_turn(turn, carry):
        @pl.when(turn < turns)
        def _():
            take_in(turn)

        @pl.when(turn == 0)
        def _():
            lay_out(LOW)
            acc[...] = jnp.zeros_like(acc)

        @pl.when(turn == 1)
        def _():
            lay_out(HIGH)
            send_other_half(0)

            @functools.partial(lax.fori_loop, 0, 2 * chips, init_val=0)
            def _(other, carry):
                @pl.when(other != blk)
                def _():
                    id_copy(other, other).wait_recv()
                return carry

            to_scalar = pltpu.make_async_copy(ids_vec, ids, id_local)
            to_scalar.start()
            to_scalar.wait()
            for m in range(row_blocks):
                add_products(core, chip, LOW, m)

        @pl.when(turn == 2)
        def _():
            for m in range(1, row_blocks):
                send_other_half(m)
            for m in range(row_blocks):
                add_products(core, chip, HIGH, m)
            for half in range(2):
                for m in range(row_blocks):
                    share_copy(sibling, chip, half, m).wait_recv()
                    add_products(sibling, chip, half, m)
            for m in range(row_blocks):
                send_partial(chip, m)

        @pl.when(turn > 2)
        def _():
            multiply(turn - 3)

        return carry

    lax.fori_loop(0, turns + 3, one_turn, 0)

    @functools.partial(lax.fori_loop, 0, chips, init_val=0)
    def _(step, carry):
        finish_distance(step)
        return carry

    def done_ids(other, carry):
        @pl.when(other != blk)
        def _():
            id_copy(blk, other).wait_send()
        return carry

    lax.fori_loop(0, 2 * chips, done_ids, 0)

    def done_source(source, carry):
        low_here = jnp.logical_or(
            source == chip,
            jnp.logical_or(
                both(source < chip, contributes(chip, source)),
                both(source == last, chip == last - 1),
            ),
        )
        high_here = jnp.logical_or(
            source == chip,
            jnp.logical_or(
                both(source > chip, contributes(chip, source)),
                both(source == 0, chip == 1),
            ),
        )
        low_sent = jnp.logical_or(
            jnp.where(source == chip, both(own_up, chip > 0), both(source < chip, chip < last)),
            both(source == chip, chip == last),
        )
        high_sent = jnp.logical_or(
            jnp.where(source == chip, both(own_down, chip < last), both(source > chip, chip > 0)),
            both(source == chip, chip == 0),
        )
        for half, here, sent in ((LOW, low_here, low_sent), (HIGH, high_here, high_sent)):
            @pl.when(here)
            def _():
                for m in range(row_blocks):
                    share_copy(core, source, half, m).wait_send()

            @pl.when(sent)
            def _():
                for m in range(row_blocks):
                    for cut in range(CUTS):
                        chain_copy(source, half, m, cut, chip).wait_send()

        @pl.when(contributes(chip, source))
        def _():
            def done_group(other, inner):
                @pl.when(other != grp)
                def _():
                    red_copy(source, grp, other).wait_send()
                return inner

            lax.fori_loop(0, groups, done_group, 0)

        return carry

    lax.fori_loop(0, chips, done_source, 0)

    mine = contributes(chip, grp)
    theirs = both(chip != grp, contributes(grp, chip))

    @pl.when(mine)
    def _():
        def wait_kept(other, carry):
            @pl.when(other != grp)
            def _():
                keep_copy(other, other).wait_recv()
            return carry

        lax.fori_loop(0, groups, wait_kept, 0)
        for core_at in range(2):
            here = slice(core_at * rows, (core_at + 1) * rows)
            out[:, here] = 0.25 * kept_sum[here, :].T

    @pl.when(theirs)
    def _():
        for core_at in range(2):
            for slot in range(per_core):
                swap_copy(chip, core_at, slot).wait_recv()

    @pl.when(both(mine, theirs))
    def _():
        for core_at in range(2):
            out[:, core_at * rows : (core_at + 1) * rows] += 0.25 * swap[core_at]

    @pl.when(jnp.logical_not(mine))
    def _():
        for core_at in range(2):
            out[:, core_at * rows : (core_at + 1) * rows] = 0.25 * swap[core_at]

    def done_sums(source, carry):
        @pl.when(contributes(chip, source))
        def _():
            @pl.when(source != chip)
            def _():
                swap_copy(source, core, 0).wait_send()

            @pl.when(source != grp)
            def _():
                keep_copy(source, grp).wait_send()

        return carry

    lax.fori_loop(0, chips, done_sums, 0)


def exchange_kernel(raw_blocks, metric_factor, sig_list, live_count):
    row_blocks, slots, width, aux = raw_blocks.shape
    blks, groups = lax.axis_size("blk"), lax.axis_size("grp")
    chips = blks // 2
    rows, part = row_blocks * width, aux // 2
    share = 2 * rows // groups
    vmem = pl.BlockSpec(memory_space=pltpu.VMEM)
    hbm = pl.BlockSpec(memory_space=pltpu.HBM)
    smem = pl.BlockSpec(memory_space=pltpu.SMEM)
    dma = pltpu.SemaphoreType.DMA
    return pl.pallas_call(
        functools.partial(kernel, chips, groups),
        out_shape=jax.ShapeDtypeStruct((rows, 2 * rows), jnp.float32),
        in_specs=[hbm, hbm, hbm, smem],
        out_specs=vmem,
        scratch_shapes=[
            pltpu.VMEM(raw_blocks.shape, jnp.bfloat16),
            pltpu.VMEM(metric_factor.shape, jnp.bfloat16),
            pltpu.VMEM(sig_list.shape, jnp.int32),
            pltpu.SMEM(sig_list.shape, jnp.int32),
            pltpu.VMEM((2, chips, 2, row_blocks, slots * width, part), jnp.bfloat16),
            pltpu.VMEM((2, slots + 1, part, rows), jnp.bfloat16),
            pltpu.VMEM((2, NOB_DEV, part, rows), jnp.bfloat16),
            pltpu.VMEM((blks, row_blocks, slots), jnp.int32),
            pltpu.SMEM((blks, row_blocks, slots), jnp.int32),
            pltpu.VMEM((chips, 2 * rows, rows), jnp.float32),
            pltpu.VMEM((chips, groups, share, rows), jnp.float32),
            pltpu.VMEM((chips, share, rows), jnp.float32),
            pltpu.VMEM((2 * rows, rows), jnp.float32),
            pltpu.VMEM((2, rows, rows), jnp.float32),
            dma((4,)), dma((blks,)), dma((blks,)), dma,
            dma((chips, 2, row_blocks, CUTS)), dma((chips, 2, row_blocks, CUTS)),
            dma((chips, 2, row_blocks)), dma((chips, 2, row_blocks)),
            dma((chips, groups)), dma((chips, groups)), dma((chips,)), dma((groups,)),
            dma((chips,)), dma((2, groups // 2)),
        ],
        compiler_params=pltpu.CompilerParams(
            collective_id=0, has_side_effects=True, vmem_limit_bytes=56400000
        ),
        cost_estimate=pl.CostEstimate(
            flops=2 * rows * 2 * rows * chips * slots * aux, bytes_accessed=2**20, transcendentals=0
        ),
    )(raw_blocks, metric_factor, sig_list, live_count.T)


def solution(mesh):
    placed = (P("blk", "grp", None, None), P(), P("blk", "grp"), P("blk", "grp"))
    return jax.shard_map(
        exchange_kernel, mesh=mesh, in_specs=placed, out_specs=P("blk", "grp"), check_vma=False
    )
```
